512 devices in a mesh: seq: 32 (over y_hi, z, core), tensor: 16 (over y_lo, x).
Axes of the slice: x: 4, y: 8 (y_hi: 2, y_lo: 4; y = y_hi * 4 + y_lo), z: 8, core: 2. Of those that a mesh axis runs over, the one named last changes fastest.
Arguments:
- tokens: bfloat16 [8192, 2304], P('seq'), may hold values from -6 to 6
- target: bfloat16 [8192, 2304], P('seq'), may hold values from -6 to 6
- segment_ids: int32 [8192], P('seq'), may hold values from 0 to 31, never falling along the last dimension, each value on 1 to 1024 neighbouring positions
- norm_gain: float32 [2304], replicated, may hold values from 0.1 to 1.9
- w_gate: bfloat16 [2304, 4608], P('seq', 'tensor'), may hold values from -0.125 to 0.125
- w_up: bfloat16 [2304, 4608], P('seq', 'tensor'), may hold values from -0.125 to 0.125
- w_down: bfloat16 [4608, 2304], P('tensor', 'seq'), may hold values from -0.09375 to 0.09375
- dir_gate: bfloat16 [2304, 4608], P('seq', 'tensor'), may hold values from -4 to 4
- dir_up: bfloat16 [2304, 4608], P('seq', 'tensor'), may hold values from -4 to 4
- dir_down: bfloat16 [4608, 2304], P('tensor', 'seq'), may hold values from -4 to 4
- ema_gate: float32 [2304, 4608], P('seq', 'tensor'), may hold values from 0.05 to 2
- ema_up: float32 [2304, 4608], P('seq', 'tensor'), may hold values from 0.05 to 2
- ema_down: float32 [4608, 2304], P('tensor', 'seq'), may hold values from 0.05 to 2
Outputs:
- new_gate: float32 [2304, 4608], P('seq', 'tensor')
- new_up: float32 [2304, 4608], P('seq', 'tensor')
- new_down: float32 [4608, 2304], P('tensor', 'seq')
The draws below stay inside these ranges and needn't reach their ends.
Inputs may be any that keep to these rules, and one draw needn't show every extreme that they name: `segment_ids`: ids never fall along the pack; each of the 32 documents has 1 to 1024 tokens, and one has exactly 1024.
All inputs are finite; a program needn't handle non-finite values.
Results may differ from the reference program's by a relative error of at most 0.025.
Values may be sent and summed in bfloat16 or wider, within the bound.
No kernel may reach another device: no remote copies, remote signals or barrier semaphores. Data moves between devices by JAX's collectives and lax.ppermute only.
A program may use at most 64 MiB of HBM per device.

```python
import math
import jax
import jax.numpy as jnp
import numpy as np
from jax import lax

D = 2304
FF = 4608
TOK_DEV = 256
TOKENS = 8192
DOCS = 32
DOC_MOST = 1024
N_TENSOR = 16


def shard_levels(own_key, shape, shards, least, top_value):
    factor_of = 1.0
    for axis_at, shards_of in shards:
        steps = jax.random.uniform(jax.random.fold_in(jax.random.fold_in(own_key, 6), axis_at), (shards_of,), jnp.float32, least / len(shards), top_value / len(shards))
        factor_of = factor_of * jnp.repeat(jnp.exp(steps), shape[axis_at] // shards_of).reshape((-1,) + (1,) * (len(shape) - 1 - axis_at))
    return factor_of


def profile(count, total, bound, skew):
    portions = [(1 << 20) // math.isqrt(grade ** skew) + 1 for grade in range(2, count + 1)]
    surplus, given = total - bound - (count - 1), [1] * (count - 1)
    while surplus > 0:
        movable = [i for i in range(count - 1) if given[i] < bound]
        pool, remaining = sum([portions[i] for i in movable]), surplus
        for i in movable:
            extra = min(bound - given[i], max(1, remaining * portions[i] // pool), surplus)
            given[i] = given[i] + extra
            surplus = surplus - extra
    return np.array([bound] + given)


def ragged(stream_key, count, total, most, skew):
    if count == 2:
        one = jax.random.randint(stream_key, (), max(1, total - most), min(most, total - 1) + 1)
        return jnp.stack([one, total - one])
    tallies = jnp.asarray(profile(count, total, most, skew), jnp.int32)
    couples = (count - 1) // 2
    source_of, sink = tallies[1:1 + 2 * couples:2], tallies[2:2 + 2 * couples:2]
    room = jnp.minimum(source_of - 1, most - sink)
    passed = jax.random.randint(jax.random.fold_in(stream_key, 1), (couples,), 0, 1 << 20) % (room + 1)
    tallies = tallies.at[1:1 + 2 * couples:2].set(source_of - passed).at[2:2 + 2 * couples:2].set(sink + passed)
    return tallies[jax.random.permutation(jax.random.fold_in(stream_key, 2), count)]


def scatter_about(key, shape, width, limit, cuts=(), kind=jnp.bfloat16):
    entries = width * jax.random.normal(key, shape, jnp.float32)
    if cuts:
        entries = entries * shard_levels(key, shape, cuts, -0.22, 0.18)
    return jnp.clip(entries, -limit, limit).astype(kind)


def setup_inputs(seed: int = 0) -> dict:
    key_of = jax.random.split(jax.random.key(seed), 14)
    tokens = scatter_about(key_of[0], (TOKENS, D), 1.0, 6.0, ((0, 32),))
    target = scatter_about(key_of[1], (TOKENS, D), 1.0, 6.0, ((0, 32),))
    segment_ids = jnp.searchsorted(jnp.cumsum(ragged(key_of[2], DOCS, TOKENS, DOC_MOST, 2)), jnp.arange(TOKENS), side="right").astype(jnp.int32)
    norm_gain = jnp.clip(1.0 + 0.18 * jax.random.normal(key_of[3], (D,), jnp.float32), 0.1, 1.9)
    w_gate = scatter_about(key_of[4], (D, FF), D ** -0.5, 0.125, ((0, 32), (1, 16)))
    w_up = scatter_about(key_of[5], (D, FF), D ** -0.5, 0.125, ((0, 32), (1, 16)))
    w_down = scatter_about(key_of[6], (FF, D), FF ** -0.5, 0.09375, ((0, 16), (1, 32)))
    dir_gate = scatter_about(key_of[7], (D, FF), 1.0, 4.0, ((0, 32), (1, 16)))
    dir_up = scatter_about(key_of[8], (D, FF), 1.0, 4.0, ((0, 32), (1, 16)))
    dir_down = scatter_about(key_of[9], (FF, D), 1.0, 4.0, ((0, 16), (1, 32)))
    ema_gate = jnp.clip(jnp.exp(math.log(2.0) - 3.6888794 * jax.random.uniform(key_of[10], (D, FF), jnp.float32) ** shard_levels(key_of[10], (D, FF), ((0, 32), (1, 16)), -0.2, 0.2)), 0.05, 2.0)
    ema_up = jnp.clip(jnp.exp(math.log(2.0) - 3.6888794 * jax.random.uniform(key_of[11], (D, FF), jnp.float32) ** shard_levels(key_of[11], (D, FF), ((0, 32), (1, 16)), -0.2, 0.2)), 0.05, 2.0)
    ema_down = jnp.clip(jnp.exp(math.log(2.0) - 3.6888794 * jax.random.uniform(key_of[12], (FF, D), jnp.float32) ** shard_levels(key_of[12], (FF, D), ((0, 16), (1, 32)), -0.2, 0.2)), 0.05, 2.0)
    return {"tokens": tokens, "target": target, "segment_ids": segment_ids, "norm_gain": norm_gain, "w_gate": w_gate, "w_up": w_up, "w_down": w_down, "dir_gate": dir_gate, "dir_up": dir_up, "dir_down": dir_down, "ema_gate": ema_gate, "ema_up": ema_up, "ema_down": ema_down}


gelu_rate = 0.7978845608028654
gelu_cubic = 0.044715
beta_decay = 0.9
norm_eps = 1e-06

def gelu_parts(pre):
    inner = gelu_rate * (pre + gelu_cubic * pre * pre * pre)
    slope = gelu_rate * (1.0 + 3.0 * gelu_cubic * pre * pre)
    bend = 6.0 * gelu_rate * gelu_cubic * pre
    tanh_val = jnp.tanh(inner)
    sech_sq = 1.0 - tanh_val * tanh_val
    value = 0.5 * pre * (1.0 + tanh_val)
    first = 0.5 * (1.0 + tanh_val) + 0.5 * pre * sech_sq * slope
    second = sech_sq * (slope + 0.5 * pre * (bend - 2.0 * tanh_val * slope * slope))
    return (value, first, second)

def normalize(tokens, norm_gain):
    wide = tokens.astype(jnp.float32)
    scale = lax.rsqrt(lax.optimization_barrier(jnp.mean(wide * wide, axis=1, keepdims=True)) + norm_eps)
    return (wide * scale * norm_gain).astype(jnp.bfloat16)

def product(left, right):
    return jnp.dot(left, right, preferred_element_type=jnp.float32)

def over_tokens(left, right):
    return lax.dot_general(left, right, (((0,), (0,)), ((), ())), preferred_element_type=jnp.float32)

def out_grads(tokens, target, mixed, mixed_dot, lengths):
    residual = tokens.astype(jnp.float32) + mixed - target.astype(jnp.float32)
    grad_out = (residual / lengths[:, None]).astype(jnp.bfloat16)
    grad_out_dot = (mixed_dot / lengths[:, None]).astype(jnp.bfloat16)
    return (grad_out, grad_out_dot)

def second_order(grad_hidden, grad_hidden_dot, upper, upper_dot, value, first, second, gate_dot):
    grad_gate_dot = ((grad_hidden_dot * upper + grad_hidden * upper_dot) * first + grad_hidden * upper * second * gate_dot).astype(jnp.bfloat16)
    grad_upper_dot = (grad_hidden_dot * value + grad_hidden * first * gate_dot).astype(jnp.bfloat16)
    return (grad_gate_dot, grad_upper_dot)

def blend(ema, probe, hvp):
    return beta_decay * ema + (1.0 - beta_decay) * (probe.astype(jnp.float32) * hvp)

def rounded(term):
    return lax.optimization_barrier(term.astype(jnp.bfloat16)).astype(jnp.float32)

def unit_sums(hidden, hidden_dot, w_down, dir_down):
    share = FF // N_TENSOR

    def by_units(array):
        return array.reshape((array.shape[0], N_TENSOR, share)).transpose((1, 0, 2))

    def by_rows(array):
        return array.reshape((N_TENSOR, share, array.shape[1]))

    def unit_step(totals, parts):
        hid_b, hdot_b, down_b, probe_b = parts
        term_mixed = rounded(product(hid_b, down_b))
        term_dot = rounded(product(hdot_b, down_b) + product(hid_b, probe_b))
        return ((totals[0] + term_mixed, totals[1] + term_dot), None)
    start = (jnp.zeros((hidden.shape[0], D), jnp.float32), jnp.zeros((hidden.shape[0], D), jnp.float32))
    totals, unused = lax.scan(unit_step, start, (by_units(hidden), by_units(hidden_dot), by_rows(w_down), by_rows(dir_down)))
    return totals

def reference(tokens, target, segment_ids, norm_gain, w_gate, w_up, w_down, dir_gate, dir_up, dir_down, ema_gate, ema_up, ema_down):
    normed = normalize(tokens, norm_gain)
    gate = product(normed, w_gate)
    upper = product(normed, w_up)
    gate_dot = product(normed, dir_gate)
    upper_dot = product(normed, dir_up)
    value, first, second = gelu_parts(gate)
    hidden = (value * upper).astype(jnp.bfloat16)
    hidden_dot = (first * gate_dot * upper + value * upper_dot).astype(jnp.bfloat16)
    mixed, mixed_dot = unit_sums(hidden, hidden_dot, w_down, dir_down)
    labels = jnp.arange(DOCS, dtype=jnp.int32)
    onehot = (segment_ids[:, None] == labels[None, :]).astype(jnp.float32)
    counts = lax.optimization_barrier(jnp.sum(onehot, axis=0))
    lengths = jnp.dot(onehot, counts, precision=lax.Precision.HIGHEST)
    grad_out, grad_out_dot = out_grads(tokens, target, mixed, mixed_dot, lengths)
    grad_hidden = lax.dot_general(grad_out, w_down, (((1,), (1,)), ((), ())), preferred_element_type=jnp.float32)
    grad_hidden_dot = lax.dot_general(grad_out_dot, w_down, (((1,), (1,)), ((), ())), preferred_element_type=jnp.float32) + lax.dot_general(grad_out, dir_down, (((1,), (1,)), ((), ())), preferred_element_type=jnp.float32)
    grad_gate_dot, grad_upper_dot = second_order(grad_hidden, grad_hidden_dot, upper, upper_dot, value, first, second, gate_dot)

    def blocks(array):
        return array.reshape((DOCS, TOK_DEV) + array.shape[1:])

    def shard_sum(totals, parts):
        normed_s, gate_s, upper_s, hdot_s, hid_s, gout_s, gdot_s = parts
        term_gate = rounded(over_tokens(normed_s, gate_s))
        term_up = rounded(over_tokens(normed_s, upper_s))
        term_down = rounded(over_tokens(hdot_s, gout_s) + over_tokens(hid_s, gdot_s))
        return ((totals[0] + term_gate, totals[1] + term_up, totals[2] + term_down), None)
    start = (jnp.zeros((D, FF), jnp.float32), jnp.zeros((D, FF), jnp.float32), jnp.zeros((FF, D), jnp.float32))
    parts = (blocks(normed), blocks(grad_gate_dot), blocks(grad_upper_dot), blocks(hidden_dot), blocks(hidden), blocks(grad_out), blocks(grad_out_dot))
    totals, unused = lax.scan(shard_sum, start, parts)
    return (blend(ema_gate, dir_gate, totals[0]), blend(ema_up, dir_up, totals[1]), blend(ema_down, dir_down, totals[2]))
```

```python
import jax
import jax.numpy as jnp
from jax import lax
from jax.sharding import PartitionSpec as P

gelu_rate = 0.7978845608028654
gelu_cubic = 0.044715
beta_decay = 0.9
norm_eps = 1e-06

NZ = 8
ROWS = 72
UNITS = 288
BF = jnp.bfloat16
F32 = jnp.float32


def gelu_parts(pre):
    inner = gelu_rate * (pre + gelu_cubic * pre * pre * pre)
    slope = gelu_rate * (1.0 + 3.0 * gelu_cubic * pre * pre)
    bend = 6.0 * gelu_rate * gelu_cubic * pre
    tanh_val = jnp.tanh(inner)
    sech_sq = 1.0 - tanh_val * tanh_val
    value = 0.5 * pre * (1.0 + tanh_val)
    first = 0.5 * (1.0 + tanh_val) + 0.5 * pre * sech_sq * slope
    second = sech_sq * (slope + 0.5 * pre * (bend - 2.0 * tanh_val * slope * slope))
    return (value, first, second)


def product(left, right):
    return jnp.dot(left, right, preferred_element_type=F32)


def against(left, right):
    return lax.dot_general(left, right, (((1,), (1,)), ((), ())), preferred_element_type=F32)


def over_tokens(left, right):
    return lax.dot_general(left, right, (((0,), (0,)), ((), ())), preferred_element_type=F32)


def blend(ema, probe, hvp):
    return beta_decay * ema + (1.0 - beta_decay) * (probe.astype(F32) * hvp)


def z_shift(array, by):
    perm = [(s, (s // 16) * 16 + ((s // 2 % 8 + by) % 8) * 2 + s % 2) for s in range(32)]
    return lax.ppermute(array, "seq", perm)


def seq_swap(array, bit):
    return lax.ppermute(array, "seq", [(s, s ^ bit) for s in range(32)])


def x_shift(array, by):
    perm = [(t, (t // 4) * 4 + (t % 4 + by) % 4) for t in range(16)]
    return lax.ppermute(array, "tensor", perm)


def y_swap(array, bit):
    return lax.ppermute(array, "tensor", [(t, t ^ (bit * 4)) for t in range(16)])


def half_of(n):
    return 128 * ((n + 255) // 256)


def gather_z(chunk, z):
    r, rows, n = chunk.shape
    h = half_of(n)
    buf = jnp.zeros((r, NZ, rows, n), chunk.dtype)

    def put(buf, piece, at, col=0):
        return lax.dynamic_update_slice(buf, piece[:, None], (0, (z + at) % NZ, 0, col))

    buf = put(buf, chunk, 0)
    up = down = chunk
    for k in (1, 2, 3):
        up = z_shift(up, 1)
        down = z_shift(down, -1)
        buf = put(buf, up, NZ - k)
        buf = put(buf, down, k)
    buf = put(buf, z_shift(up[:, :, :h], 1), 4)
    buf = put(buf, z_shift(down[:, :, h:], -1), 4, h)
    return buf


def scatter_z(parts, z):
    n = parts.shape[-1]
    h = half_of(n)

    def block(at):
        return lax.dynamic_index_in_dim(parts, (z + at) % NZ, 0, keepdims=False)

    def add(left, right):
        return (left.astype(F32) + right.astype(F32)).astype(BF)

    far = block(4)
    up, down = z_shift(far[:, :h], 1), z_shift(far[:, h:], -1)
    ahead, behind = block(3), block(5)
    up = jnp.concatenate([add(ahead[:, :h], up), ahead[:, h:]], axis=1)
    down = jnp.concatenate([behind[:, :h], add(behind[:, h:], down)], axis=1)
    for k in (2, 1):
        up, down = add(block(k), z_shift(up, 1)), add(block(NZ - k), z_shift(down, -1))
    up, down = z_shift(up, 1), z_shift(down, -1)
    return block(0).astype(F32) + up.astype(F32) + down.astype(F32)


def scatter_tensor(part, x, y):
    n = part.shape[1]
    h = n // 2
    part = part.reshape(4, 64, n)

    def block(at):
        return lax.dynamic_index_in_dim(part, (x + at) % 4, 0, keepdims=False)

    def add(left, right):
        return (left.astype(F32) + right.astype(F32)).astype(BF)

    far, ahead, behind = block(2), block(1), block(3)
    up, down = x_shift(far[:, :h], 1), x_shift(far[:, h:], -1)
    up = x_shift(jnp.concatenate([add(ahead[:, :h], up), ahead[:, h:]], axis=1), 1)
    down = x_shift(jnp.concatenate([behind[:, :h], add(behind[:, h:], down)], axis=1), -1)
    total = block(0).astype(F32) + up.astype(F32) + down.astype(F32)
    total = total.reshape(2, 2, 16, n)
    low = y % 2
    mine = lax.dynamic_index_in_dim(total, low, 1, keepdims=False)
    other = lax.dynamic_index_in_dim(total, 1 - low, 1, keepdims=False).astype(BF)
    mine = mine + y_swap(other, 1).astype(F32)
    high = y // 2
    own = lax.dynamic_index_in_dim(mine, high, 0, keepdims=False)
    other = lax.dynamic_index_in_dim(mine, 1 - high, 0, keepdims=False).astype(BF)
    return own + y_swap(other, 2).astype(F32)


def gather_tensor(own, x, y):
    n = own.shape[1]
    h = n // 2
    low, high = y % 2, y // 2
    other = y_swap(own, 2)
    pair = jnp.where(high == 0, jnp.stack([own, other]), jnp.stack([other, own]))
    other = y_swap(pair, 1)
    rows = jnp.where(low == 0, jnp.stack([pair, other], axis=1), jnp.stack([other, pair], axis=1))
    rows = rows.reshape(64, n)
    buf = jnp.zeros((4, 64, n), own.dtype)

    def put(buf, piece, at, col=0):
        return lax.dynamic_update_slice(buf, piece[None], ((x + at) % 4, 0, col))

    buf = put(buf, rows, 0)
    up, down = x_shift(rows, 1), x_shift(rows, -1)
    buf = put(put(buf, up, 3), down, 1)
    buf = put(buf, x_shift(up[:, :h], 1), 2)
    buf = put(buf, x_shift(down[:, h:], -1), 2, h)
    return buf.reshape(256, n)


def relative(rows, y, c):
    m = rows.shape[0]
    parts = rows.reshape(m, 2, NZ, 2, ROWS).transpose(1, 3, 0, 2, 4).reshape(2, 2, m, NZ * ROWS)
    parts = jnp.where(y == 0, parts, parts[::-1])
    parts = jnp.where(c == 0, parts, parts[:, ::-1])
    return parts.transpose(2, 0, 1, 3).reshape(m, 4 * NZ * ROWS)


def per_device(
    tokens,
    target,
    segment_ids,
    norm_gain,
    w_gate,
    w_up,
    w_down,
    dir_gate,
    dir_up,
    dir_down,
    ema_gate,
    ema_up,
    ema_down,
):
    s = lax.axis_index("seq")
    t = lax.axis_index("tensor")
    yh, z, c = s // 16, (s // 2) % 8, s % 2
    yl, x = t // 4, t % 4

    own_in = jnp.concatenate([w_gate, w_up, dir_gate, dir_up], axis=1)[None]
    own_out = jnp.concatenate([w_down.T, dir_down.T], axis=1)[None]
    across_in = seq_swap(own_in, 16)
    across_out = seq_swap(own_out, 16)
    near = gather_z(own_in, z)
    near_other = seq_swap(near, 1)
    away = gather_z(across_in, z)
    away_other = seq_swap(away, 1)
    outs = gather_z(jnp.concatenate([own_out, across_out], axis=0), z)
    outs_other = seq_swap(outs, 1)

    def joined(mine, other):
        return jnp.concatenate([mine[0], other[0]], axis=0).reshape(2 * NZ * ROWS, mine.shape[-1])

    labels = jnp.arange(32, dtype=jnp.int32)
    onehot = (segment_ids[:, None] == labels[None, :]).astype(F32)
    counts = jnp.sum(onehot, axis=0, keepdims=True)
    for bit in (1, 2, 4, 8, 16):
        counts = counts + seq_swap(counts, bit)

    wide = tokens.astype(F32)
    scale = lax.rsqrt(jnp.mean(wide * wide, axis=1, keepdims=True) + norm_eps)
    normed = (wide * scale * norm_gain).astype(BF)
    normed = relative(normed, yh, c)

    half = 2 * NZ * ROWS
    pre = product(normed[:, :half], joined(near, near_other)) + product(
        normed[:, half:], joined(away, away_other)
    )
    gate, upper, gate_dot, upper_dot = (pre[:, i * UNITS : (i + 1) * UNITS] for i in range(4))
    value, first, second = gelu_parts(gate)
    hidden = (value * upper).astype(BF)
    hidden_dot = (first * gate_dot * upper + value * upper_dot).astype(BF)

    down_all = jnp.stack([outs, outs_other], axis=1).reshape(4 * NZ * ROWS, 2 * UNITS)
    mixed_part = against(hidden, down_all[:, :UNITS]).astype(BF)
    mixed_dot_part = against(jnp.concatenate([hidden_dot, hidden], axis=1), down_all).astype(BF)

    mixed = scatter_tensor(mixed_part, x, yl)
    mixed_dot = scatter_tensor(mixed_dot_part, x, yl)

    at = x * 64 + yl * 16
    my_tokens = relative(lax.dynamic_slice_in_dim(tokens, at, 16, 0), yh, c).astype(F32)
    my_target = relative(lax.dynamic_slice_in_dim(target, at, 16, 0), yh, c).astype(F32)
    my_hot = lax.dynamic_slice_in_dim(onehot, at, 16, 0)
    lengths = jnp.sum(my_hot * counts, axis=1, keepdims=True)
    my_grad = ((my_tokens + mixed - my_target) / lengths).astype(BF)
    my_grad_dot = (mixed_dot / lengths).astype(BF)
    grad_out = gather_tensor(my_grad, x, yl)
    grad_out_dot = gather_tensor(my_grad_dot, x, yl)

    back = product(grad_out, down_all)
    back_dot = product(grad_out_dot, down_all[:, :UNITS])
    grad_hidden = back[:, :UNITS]
    grad_hidden_dot = back_dot + back[:, UNITS:]
    grad_gate_dot = (
        (grad_hidden_dot * upper + grad_hidden * upper_dot) * first
        + grad_hidden * upper * second * gate_dot
    ).astype(BF)
    grad_upper_dot = (grad_hidden_dot * value + grad_hidden * first * gate_dot).astype(BF)
    grads = jnp.concatenate([grad_gate_dot, grad_upper_dot], axis=1)

    def terms(lo):
        part_in = over_tokens(normed[:, lo : lo + half], grads).astype(BF)
        part_out = (
            over_tokens(grad_out[:, lo : lo + half], hidden_dot)
            + over_tokens(grad_out_dot[:, lo : lo + half], hidden)
        ).astype(BF)
        part = jnp.concatenate([part_in, part_out], axis=1).reshape(2, NZ, ROWS, 3 * UNITS)
        return (part[0].astype(F32) + seq_swap(part[1], 1).astype(F32)).astype(BF)

    far_sum = scatter_z(terms(half), z)
    far_sum = seq_swap(far_sum.astype(BF), 16).astype(F32)
    hvp = scatter_z(terms(0), z) + far_sum
    return (
        blend(ema_gate, dir_gate, hvp[:, :UNITS]),
        blend(ema_up, dir_up, hvp[:, UNITS : 2 * UNITS]),
        blend(ema_down, dir_down, hvp[:, 2 * UNITS :].T),
    )


def solution(mesh):
    in_specs = (
        P("seq", None),
        P("seq", None),
        P("seq"),
        P(),
        P("seq", "tensor"),
        P("seq", "tensor"),
        P("tensor", "seq"),
        P("seq", "tensor"),
        P("seq", "tensor"),
        P("tensor", "seq"),
        P("seq", "tensor"),
        P("seq", "tensor"),
        P("tensor", "seq"),
    )
    out_specs = (P("seq", "tensor"), P("seq", "tensor"), P("tensor", "seq"))
    return jax.shard_map(
        per_device, mesh=mesh, in_specs=in_specs, out_specs=out_specs, check_vma=False
    )
```

```python
import jax
import jax.numpy as jnp
from jax import lax
from jax.sharding import PartitionSpec as P

gelu_rate = 0.7978845608028654
gelu_cubic = 0.044715
beta_decay = 0.9
norm_eps = 1e-06

NZ = 8
ROWS = 72
UNITS = 288
TALLY = 64
BF = jnp.bfloat16
F32 = jnp.float32


def gelu_parts(pre):
    inner = gelu_rate * (pre + gelu_cubic * pre * pre * pre)
    slope = gelu_rate * (1.0 + 3.0 * gelu_cubic * pre * pre)
    bend = 6.0 * gelu_rate * gelu_cubic * pre
    tanh_val = jnp.tanh(inner)
    sech_sq = 1.0 - tanh_val * tanh_val
    value = 0.5 * pre * (1.0 + tanh_val)
    first = 0.5 * (1.0 + tanh_val) + 0.5 * pre * sech_sq * slope
    second = sech_sq * (slope + 0.5 * pre * (bend - 2.0 * tanh_val * slope * slope))
    return (value, first, second)


def product(left, right):
    return jnp.dot(left, right, preferred_element_type=F32)


def against(left, right):
    return lax.dot_general(left, right, (((1,), (1,)), ((), ())), preferred_element_type=F32)


def over_tokens(left, right):
    return lax.dot_general(left, right, (((0,), (0,)), ((), ())), preferred_element_type=F32)


def blend(ema, probe, hvp):
    return beta_decay * ema + (1.0 - beta_decay) * (probe.astype(F32) * hvp)


def ring_step(array):
    perm = [
        (s, (s // 16) * 16 + ((s // 2 % 8 + (1 - 2 * (s % 2))) % 8) * 2 + s % 2) for s in range(32)
    ]
    return lax.ppermute(array, "seq", perm)


def seq_swap(array, bit):
    return lax.ppermute(array, "seq", [(s, s ^ bit) for s in range(32)])


def y_swap(array, bit):
    return lax.ppermute(array, "tensor", [(t, t ^ (bit * 4)) for t in range(16)])


Z_GROUPS = [[y * 16 + z * 2 + c for z in range(8)] for y in range(2) for c in range(2)]
X_GROUPS = [[y * 4 + x for x in range(4)] for y in range(4)]
Y_GROUPS = [[y * 4 + x for y in range(4)] for x in range(4)]


def group_gather(array, axis, groups):
    return lax.all_gather(array, axis, axis_index_groups=groups)


def group_scatter(array, axis, groups):
    return lax.psum_scatter(array, axis, scatter_dimension=0, axis_index_groups=groups)


def group_exchange(array, axis, groups):
    return lax.all_to_all(array, axis, 0, 0, axis_index_groups=groups)


def gather_ring(chunk, z, sign):
    r, rows, n = chunk.shape
    own = jnp.zeros((r, NZ, rows, n), chunk.dtype)
    other = jnp.zeros((r, NZ, rows, n), chunk.dtype)
    held = chunk
    for k in range(NZ):
        nxt = ring_step(held) if k < NZ - 1 else None
        own = lax.dynamic_update_slice(own, held[:, None], (0, (z - sign * k) % NZ, 0, 0))
        across = seq_swap(held, 1)
        other = lax.dynamic_update_slice(other, across[:, None], (0, (z + sign * k) % NZ, 0, 0))
        held = nxt
    return own, other


def scatter_ring(parts, z, sign):
    def block(at):
        return lax.dynamic_index_in_dim(parts, (z + sign * at) % NZ, 0, keepdims=False)

    held = ring_step(block(7))
    for k in range(6, 0, -1):
        held = ring_step((block(k).astype(F32) + held.astype(F32)).astype(BF))
    return block(0).astype(F32) + held.astype(F32)


def scatter_tensor(part, x, y):
    n = part.shape[1]
    got = group_exchange(part.reshape(4, 64, n), "tensor", X_GROUPS)
    total = jnp.sum(got.astype(F32), axis=0).astype(BF)
    got = group_exchange(total.reshape(4, 16, n), "tensor", Y_GROUPS)
    return jnp.sum(got.astype(F32), axis=0)


def gather_tensor(own, x, y):
    n = own.shape[1]
    low, high = y % 2, y // 2
    other = y_swap(own, 2)
    pair = jnp.where(high == 0, jnp.stack([own, other]), jnp.stack([other, own]))
    other = y_swap(pair, 1)
    rows = jnp.where(low == 0, jnp.stack([pair, other], axis=1), jnp.stack([other, pair], axis=1))
    return group_gather(rows.reshape(64, n), "tensor", X_GROUPS).reshape(256, n)


def relative(rows, y, c):
    m = rows.shape[0]
    parts = rows.reshape(m, 2, NZ, 2, ROWS).transpose(1, 3, 0, 2, 4).reshape(2, 2, m, NZ * ROWS)
    parts = jnp.where(y == 0, parts, parts[::-1])
    parts = jnp.where(c == 0, parts, parts[:, ::-1])
    return parts.transpose(2, 0, 1, 3).reshape(m, 4 * NZ * ROWS)


def per_device(
    tokens,
    target,
    segment_ids,
    norm_gain,
    w_gate,
    w_up,
    w_down,
    dir_gate,
    dir_up,
    dir_down,
    ema_gate,
    ema_up,
    ema_down,
):
    s = lax.axis_index("seq")
    t = lax.axis_index("tensor")
    yh, z, c = s // 16, (s // 2) % 8, s % 2
    yl, x = t // 4, t % 4

    sign = 1 - 2 * c
    labels = jnp.arange(32, dtype=jnp.int32)
    onehot = (segment_ids[:, None] == labels[None, :]).astype(F32)

    own_in = jnp.concatenate([w_gate, w_up, dir_gate, dir_up], axis=1)
    tally = jnp.pad(jnp.sum(onehot, axis=0).astype(BF)[None], ((0, ROWS - 1), (0, TALLY - 32)))
    own_out = jnp.concatenate([w_down.T, dir_down.T, tally], axis=1)
    pair_in = jnp.stack([own_in, seq_swap(own_in, 16)])
    pair_out = jnp.stack([own_out, seq_swap(own_out, 16)])
    outs = group_gather(pair_out, "seq", Z_GROUPS).transpose(1, 0, 2, 3)
    ins, ins_other = gather_ring(pair_in, z, sign)
    outs_other = seq_swap(outs, 1)

    wide = tokens.astype(F32)
    scale = lax.rsqrt(jnp.mean(wide * wide, axis=1, keepdims=True) + norm_eps)
    normed = (wide * scale * norm_gain).astype(BF)
    normed = relative(normed, yh, c)

    half = 2 * NZ * ROWS
    ins_all = jnp.stack([ins, ins_other], axis=1).reshape(2, half, 4 * UNITS)
    pre = product(normed[:, :half], ins_all[0]) + product(normed[:, half:], ins_all[1])
    gate, upper, gate_dot, upper_dot = (pre[:, i * UNITS : (i + 1) * UNITS] for i in range(4))
    value, first, second = gelu_parts(gate)
    hidden = (value * upper).astype(BF)
    hidden_dot = (first * gate_dot * upper + value * upper_dot).astype(BF)

    outs_all = jnp.stack([outs, outs_other], axis=1)
    counts = jnp.sum(outs_all[:, :, :, 0, 2 * UNITS : 2 * UNITS + 32].astype(F32), axis=(0, 1, 2))
    down_all = outs_all[..., : 2 * UNITS].reshape(4 * NZ * ROWS, 2 * UNITS)
    mixed_part = against(hidden, down_all[:, :UNITS]).astype(BF)
    mixed_dot_part = against(jnp.concatenate([hidden_dot, hidden], axis=1), down_all).astype(BF)
    width = 4 * NZ * ROWS
    sums = scatter_tensor(jnp.concatenate([mixed_part, mixed_dot_part], axis=1), x, yl)
    mixed, mixed_dot = sums[:, :width], sums[:, width:]

    at = x * 64 + yl * 16
    my_tokens = relative(lax.dynamic_slice_in_dim(tokens, at, 16, 0), yh, c).astype(F32)
    my_target = relative(lax.dynamic_slice_in_dim(target, at, 16, 0), yh, c).astype(F32)
    my_hot = lax.dynamic_slice_in_dim(onehot, at, 16, 0)
    lengths = jnp.sum(my_hot * counts[None], axis=1, keepdims=True)
    my_grad = ((my_tokens + mixed - my_target) / lengths).astype(BF)
    my_grad_dot = (mixed_dot / lengths).astype(BF)
    grads_out = gather_tensor(jnp.concatenate([my_grad, my_grad_dot], axis=1), x, yl)
    grad_out, grad_out_dot = grads_out[:, :width], grads_out[:, width:]

    back = product(grad_out, down_all)
    back_dot = product(grad_out_dot, down_all[:, :UNITS])
    grad_hidden = back[:, :UNITS]
    grad_hidden_dot = back_dot + back[:, UNITS:]
    grad_gate_dot = (
        (grad_hidden_dot * upper + grad_hidden * upper_dot) * first
        + grad_hidden * upper * second * gate_dot
    ).astype(BF)
    grad_upper_dot = (grad_hidden_dot * value + grad_hidden * first * gate_dot).astype(BF)
    grads = jnp.concatenate([grad_gate_dot, grad_upper_dot], axis=1)

    part_in = over_tokens(normed, grads).astype(BF)
    part_out = (over_tokens(grad_out, hidden_dot) + over_tokens(grad_out_dot, hidden)).astype(BF)

    def core_sum(part):
        part = part.reshape(2, 2, NZ, ROWS, part.shape[1])
        part = (part[:, 0].astype(F32) + seq_swap(part[:, 1], 1).astype(F32)).astype(BF)
        return part.transpose(1, 0, 2, 3)

    sum_out = group_scatter(core_sum(part_out), "seq", Z_GROUPS).astype(F32)
    sum_in = scatter_ring(core_sum(part_in), z, sign)
    sums = jnp.concatenate([sum_in, sum_out], axis=2)
    hvp = sums[0] + seq_swap(sums[1].astype(BF), 16).astype(F32)
    return (
        blend(ema_gate, dir_gate, hvp[:, :UNITS]),
        blend(ema_up, dir_up, hvp[:, UNITS : 2 * UNITS]),
        blend(ema_down, dir_down, hvp[:, 2 * UNITS :].T),
    )


def solution(mesh):
    in_specs = (
        P("seq", None),
        P("seq", None),
        P("seq"),
        P(),
        P("seq", "tensor"),
        P("seq", "tensor"),
        P("tensor", "seq"),
        P("seq", "tensor"),
        P("seq", "tensor"),
        P("tensor", "seq"),
        P("seq", "tensor"),
        P("seq", "tensor"),
        P("tensor", "seq"),
    )
    out_specs = (P("seq", "tensor"), P("seq", "tensor"), P("tensor", "seq"))
    return jax.shard_map(
        per_device, mesh=mesh, in_specs=in_specs, out_specs=out_specs, check_vma=False
    )
```

```python
import jax
import jax.numpy as jnp
from jax import lax
from jax.sharding import PartitionSpec as P

gelu_rate = 0.7978845608028654
gelu_cubic = 0.044715
beta_decay = 0.9
norm_eps = 1e-06

NZ = 8
ROWS = 72
UNITS = 288
TALLY = 64
BF = jnp.bfloat16
F32 = jnp.float32


def gelu_parts(pre):
    inner = gelu_rate * (pre + gelu_cubic * pre * pre * pre)
    slope = gelu_rate * (1.0 + 3.0 * gelu_cubic * pre * pre)
    bend = 6.0 * gelu_rate * gelu_cubic * pre
    tanh_val = jnp.tanh(inner)
    sech_sq = 1.0 - tanh_val * tanh_val
    value = 0.5 * pre * (1.0 + tanh_val)
    first = 0.5 * (1.0 + tanh_val) + 0.5 * pre * sech_sq * slope
    second = sech_sq * (slope + 0.5 * pre * (bend - 2.0 * tanh_val * slope * slope))
    return (value, first, second)


def product(left, right):
    return jnp.dot(left, right, preferred_element_type=F32)


def against(left, right):
    return lax.dot_general(left, right, (((1,), (1,)), ((), ())), preferred_element_type=F32)


def over_tokens(left, right):
    return lax.dot_general(left, right, (((0,), (0,)), ((), ())), preferred_element_type=F32)


def blend(ema, probe, hvp):
    return beta_decay * ema + (1.0 - beta_decay) * (probe.astype(F32) * hvp)


def ring_step(array):
    perm = [
        (s, (s // 16) * 16 + ((s // 2 % 8 + (1 - 2 * (s % 2))) % 8) * 2 + s % 2) for s in range(32)
    ]
    return lax.ppermute(array, "seq", perm)


def seq_swap(array, bit):
    return lax.ppermute(array, "seq", [(s, s ^ bit) for s in range(32)])


def y_swap(array, bit):
    return lax.ppermute(array, "tensor", [(t, t ^ (bit * 4)) for t in range(16)])


Z_GROUPS = [[y * 16 + z * 2 + c for z in range(8)] for y in range(2) for c in range(2)]
X_GROUPS = [[y * 4 + x for x in range(4)] for y in range(4)]
Y_GROUPS = [[y * 4 + x for y in range(4)] for x in range(4)]


def group_gather(array, axis, groups):
    return lax.all_gather(array, axis, axis_index_groups=groups)


def group_scatter(array, axis, groups):
    return lax.psum_scatter(array, axis, scatter_dimension=0, axis_index_groups=groups)


def group_exchange(array, axis, groups):
    return lax.all_to_all(array, axis, 0, 0, axis_index_groups=groups)


def gather_ring(chunk, z, sign):
    own = jnp.zeros((NZ,) + chunk.shape, chunk.dtype)
    held = chunk
    for k in range(NZ):
        own = lax.dynamic_update_slice(own, held[None], ((z - sign * k) % NZ, 0, 0))
        held = ring_step(held) if k < NZ - 1 else None
    return own


def exchange_sum(parts, axis, groups):
    return jnp.sum(group_exchange(parts, axis, groups).astype(F32), axis=0)


def share(own, groups):
    return group_exchange(jnp.broadcast_to(own[None], (4,) + own.shape), "tensor", groups)


def scatter_tensor(part):
    n = part.shape[1]
    cut = n * 3 // 4
    part = part.reshape(4, 4, 16, n)
    left = part[..., :cut].reshape(4, 64, cut)
    right = part[..., cut:].transpose(1, 0, 2, 3).reshape(4, 64, n - cut)
    left = exchange_sum(left, "tensor", X_GROUPS).astype(BF).reshape(4, 16, cut)
    right = exchange_sum(right, "tensor", Y_GROUPS).astype(BF).reshape(4, 16, n - cut)
    left = exchange_sum(left, "tensor", Y_GROUPS)
    right = exchange_sum(right, "tensor", X_GROUPS)
    return jnp.concatenate([left, right], axis=1)


def gather_tensor(own):
    n = own.shape[1]
    cut = n * 3 // 4
    left, right = own[:, :cut], own[:, cut:]
    left = share(left, Y_GROUPS).reshape(64, cut)
    right = share(right, X_GROUPS).reshape(64, n - cut)
    left = share(left, X_GROUPS).reshape(256, cut)
    right = share(right, Y_GROUPS).reshape(4, 4, 16, n - cut)
    right = right.transpose(1, 0, 2, 3).reshape(256, n - cut)
    return jnp.concatenate([left, right], axis=1)


def relative(rows, y, c):
    m = rows.shape[0]
    parts = rows.reshape(m, 2, NZ, 2, ROWS).transpose(1, 3, 0, 2, 4).reshape(2, 2, m, NZ * ROWS)
    parts = jnp.where(y == 0, parts, parts[::-1])
    parts = jnp.where(c == 0, parts, parts[:, ::-1])
    return parts.transpose(2, 0, 1, 3).reshape(m, 4 * NZ * ROWS)


def per_device(
    tokens,
    target,
    segment_ids,
    norm_gain,
    w_gate,
    w_up,
    w_down,
    dir_gate,
    dir_up,
    dir_down,
    ema_gate,
    ema_up,
    ema_down,
):
    s = lax.axis_index("seq")
    t = lax.axis_index("tensor")
    yh, z, c = s // 16, (s // 2) % 8, s % 2
    yl, x = t // 4, t % 4

    sign = 1 - 2 * c
    labels = jnp.arange(32, dtype=jnp.int32)
    onehot = (segment_ids[:, None] == labels[None, :]).astype(F32)

    own_in = jnp.concatenate([w_gate, w_up, dir_gate, dir_up], axis=1)
    tally = jnp.pad(jnp.sum(onehot, axis=0).astype(BF)[None], ((0, ROWS - 1), (0, TALLY - 32)))
    own_out = jnp.concatenate([w_down.T, dir_down.T, tally], axis=1)
    across_in = seq_swap(own_in, 16)
    near = gather_ring(own_in, z, sign)
    across_out = seq_swap(own_out, 16)
    outs_near = group_gather(own_out, "seq", Z_GROUPS)
    outs_away = group_gather(across_out, "seq", Z_GROUPS)
    near_other = seq_swap(near, 1)
    away = gather_ring(across_in, z, sign)
    away_other = seq_swap(away, 1)
    outs_near_other = seq_swap(outs_near, 1)
    outs_away_other = seq_swap(outs_away, 1)

    wide = tokens.astype(F32)
    scale = lax.rsqrt(jnp.mean(wide * wide, axis=1, keepdims=True) + norm_eps)
    normed = (wide * scale * norm_gain).astype(BF)
    normed = relative(normed, yh, c)

    half = 2 * NZ * ROWS
    near_all = jnp.stack([near, near_other]).reshape(half, 4 * UNITS)
    away_all = jnp.stack([away, away_other]).reshape(half, 4 * UNITS)
    pre = product(normed[:, :half], near_all) + product(normed[:, half:], away_all)
    gate, upper, gate_dot, upper_dot = (pre[:, i * UNITS : (i + 1) * UNITS] for i in range(4))
    value, first, second = gelu_parts(gate)
    hidden = (value * upper).astype(BF)
    hidden_dot = (first * gate_dot * upper + value * upper_dot).astype(BF)

    outs_all = jnp.stack([outs_near, outs_near_other, outs_away, outs_away_other])
    counts = jnp.sum(outs_all[:, :, 0, 2 * UNITS : 2 * UNITS + 32].astype(F32), axis=(0, 1))
    down_all = outs_all[..., : 2 * UNITS].reshape(4 * NZ * ROWS, 2 * UNITS)
    mixed_part = against(hidden, down_all[:, :UNITS]).astype(BF)
    mixed_dot_part = against(jnp.concatenate([hidden_dot, hidden], axis=1), down_all).astype(BF)
    width = 4 * NZ * ROWS
    sums = scatter_tensor(jnp.concatenate([mixed_part, mixed_dot_part], axis=1))
    mixed, mixed_dot = sums[:, :width], sums[:, width:]

    at = x * 64 + yl * 16
    my_tokens = relative(lax.dynamic_slice_in_dim(tokens, at, 16, 0), yh, c).astype(F32)
    my_target = relative(lax.dynamic_slice_in_dim(target, at, 16, 0), yh, c).astype(F32)
    my_hot = lax.dynamic_slice_in_dim(onehot, at, 16, 0)
    lengths = jnp.sum(my_hot * counts[None], axis=1, keepdims=True)
    my_grad = ((my_tokens + mixed - my_target) / lengths).astype(BF)
    my_grad_dot = (mixed_dot / lengths).astype(BF)
    grads_out = gather_tensor(jnp.concatenate([my_grad, my_grad_dot], axis=1))
    grad_out, grad_out_dot = grads_out[:, :width], grads_out[:, width:]

    back = product(grad_out, down_all)
    back_dot = product(grad_out_dot, down_all[:, :UNITS])
    grad_hidden = back[:, :UNITS]
    grad_hidden_dot = back_dot + back[:, UNITS:]
    grad_gate_dot = (
        (grad_hidden_dot * upper + grad_hidden * upper_dot) * first
        + grad_hidden * upper * second * gate_dot
    ).astype(BF)
    grad_upper_dot = (grad_hidden_dot * value + grad_hidden * first * gate_dot).astype(BF)
    grads = jnp.concatenate([grad_gate_dot, grad_upper_dot], axis=1)

    def terms(lo):
        rows = slice(lo, lo + half)
        part_in = over_tokens(normed[:, rows], grads).astype(BF)
        part_out = (
            over_tokens(grad_out[:, rows], hidden_dot) + over_tokens(grad_out_dot[:, rows], hidden)
        ).astype(BF)
        part = jnp.concatenate([part_in, part_out], axis=1).reshape(2, NZ, ROWS, 3 * UNITS)
        return (part[0].astype(F32) + seq_swap(part[1], 1).astype(F32)).astype(BF)

    away_terms = terms(half)
    near_terms = terms(0)
    away_sum = exchange_sum(away_terms, "seq", Z_GROUPS).astype(BF)
    away_sum = seq_swap(away_sum, 16).astype(F32)
    near_tail = group_scatter(near_terms[..., UNITS:], "seq", Z_GROUPS).astype(F32)
    near_head = exchange_sum(near_terms[..., :UNITS], "seq", Z_GROUPS)
    hvp = jnp.concatenate([near_head, near_tail], axis=1) + away_sum
    return (
        blend(ema_gate, dir_gate, hvp[:, :UNITS]),
        blend(ema_up, dir_up, hvp[:, UNITS : 2 * UNITS]),
        blend(ema_down, dir_down, hvp[:, 2 * UNITS :].T),
    )


def solution(mesh):
    in_specs = (
        P("seq", None),
        P("seq", None),
        P("seq"),
        P(),
        P("seq", "tensor"),
        P("seq", "tensor"),
        P("tensor", "seq"),
        P("seq", "tensor"),
        P("seq", "tensor"),
        P("tensor", "seq"),
        P("seq", "tensor"),
        P("seq", "tensor"),
        P("tensor", "seq"),
    )
    out_specs = (P("seq", "tensor"), P("seq", "tensor"), P("tensor", "seq"))
    return jax.shard_map(
        per_device, mesh=mesh, in_specs=in_specs, out_specs=out_specs, check_vma=False
    )
```

```python
import jax
import jax.numpy as jnp
from jax import lax
from jax.sharding import PartitionSpec as P

gelu_rate = 0.7978845608028654
gelu_cubic = 0.044715
beta_decay = 0.9
norm_eps = 1e-06

NZ = 8
ROWS = 72
UNITS = 288
TALLY = 64
BF = jnp.bfloat16
F32 = jnp.float32


def gelu_parts(pre):
    inner = gelu_rate * (pre + gelu_cubic * pre * pre * pre)
    slope = gelu_rate * (1.0 + 3.0 * gelu_cubic * pre * pre)
    bend = 6.0 * gelu_rate * gelu_cubic * pre
    tanh_val = jnp.tanh(inner)
    sech_sq = 1.0 - tanh_val * tanh_val
    value = 0.5 * pre * (1.0 + tanh_val)
    first = 0.5 * (1.0 + tanh_val) + 0.5 * pre * sech_sq * slope
    second = sech_sq * (slope + 0.5 * pre * (bend - 2.0 * tanh_val * slope * slope))
    return (value, first, second)


def product(left, right):
    return jnp.dot(left, right, preferred_element_type=F32)


def against(left, right):
    return lax.dot_general(left, right, (((1,), (1,)), ((), ())), preferred_element_type=F32)


def over_tokens(left, right):
    return lax.dot_general(left, right, (((0,), (0,)), ((), ())), preferred_element_type=F32)


def blend(ema, probe, hvp):
    return beta_decay * ema + (1.0 - beta_decay) * (probe.astype(F32) * hvp)


def ring_step(array):
    perm = [
        (s, (s // 16) * 16 + ((s // 2 % 8 + (1 - 2 * (s % 2))) % 8) * 2 + s % 2) for s in range(32)
    ]
    return lax.ppermute(array, "seq", perm)


def seq_swap(array, bit):
    return lax.ppermute(array, "seq", [(s, s ^ bit) for s in range(32)])


def y_swap(array, bit):
    return lax.ppermute(array, "tensor", [(t, t ^ (bit * 4)) for t in range(16)])


Z_GROUPS = [[y * 16 + z * 2 + c for z in range(8)] for y in range(2) for c in range(2)]
X_GROUPS = [[y * 4 + x for x in range(4)] for y in range(4)]
Y_GROUPS = [[y * 4 + x for y in range(4)] for x in range(4)]


def group_gather(array, axis, groups):
    return lax.all_gather(array, axis, axis_index_groups=groups)


def group_scatter(array, axis, groups):
    return lax.psum_scatter(array, axis, scatter_dimension=0, axis_index_groups=groups)


def group_exchange(array, axis, groups):
    return lax.all_to_all(array, axis, 0, 0, axis_index_groups=groups)


def gather_ring(chunk, z, sign):
    own = jnp.zeros((NZ,) + chunk.shape, chunk.dtype)
    held = chunk
    for k in range(NZ):
        own = lax.dynamic_update_slice(own, held[None], ((z - sign * k) % NZ, 0, 0))
        held = ring_step(held) if k < NZ - 1 else None
    return own


def exchange_sum(parts, axis, groups):
    return jnp.sum(group_exchange(parts, axis, groups).astype(F32), axis=0)


def x_shift(array, by):
    perm = [(t, (t // 4) * 4 + (t % 4 + by) % 4) for t in range(16)]
    return lax.ppermute(array, "tensor", perm)


def scatter_tensor(part, x, y):
    n = part.shape[1]
    h = n // 2
    part = part.reshape(4, 64, n)

    def block(at):
        return lax.dynamic_index_in_dim(part, (x + at) % 4, 0, keepdims=False)

    def add(left, right):
        return (left.astype(F32) + right.astype(F32)).astype(BF)

    far, ahead, behind = block(2), block(1), block(3)
    up, down = x_shift(far[:, :h], 1), x_shift(far[:, h:], -1)
    up = x_shift(jnp.concatenate([add(ahead[:, :h], up), ahead[:, h:]], axis=1), 1)
    down = x_shift(jnp.concatenate([behind[:, :h], add(behind[:, h:], down)], axis=1), -1)
    total = block(0).astype(F32) + up.astype(F32) + down.astype(F32)
    total = total.reshape(2, 2, 16, n)
    low = y % 2
    mine = lax.dynamic_index_in_dim(total, low, 1, keepdims=False)
    other = lax.dynamic_index_in_dim(total, 1 - low, 1, keepdims=False).astype(BF)
    mine = mine + y_swap(other, 1).astype(F32)
    high = y // 2
    own = lax.dynamic_index_in_dim(mine, high, 0, keepdims=False)
    other = lax.dynamic_index_in_dim(mine, 1 - high, 0, keepdims=False).astype(BF)
    return own + y_swap(other, 2).astype(F32)


def gather_tensor(own, x, y):
    n = own.shape[1]
    h = n // 2
    low, high = y % 2, y // 2
    other = y_swap(own, 2)
    pair = jnp.where(high == 0, jnp.stack([own, other]), jnp.stack([other, own]))
    other = y_swap(pair, 1)
    rows = jnp.where(low == 0, jnp.stack([pair, other], axis=1), jnp.stack([other, pair], axis=1))
    rows = rows.reshape(64, n)
    buf = jnp.zeros((4, 64, n), own.dtype)

    def put(buf, piece, at, col=0):
        return lax.dynamic_update_slice(buf, piece[None], ((x + at) % 4, 0, col))

    buf = put(buf, rows, 0)
    up, down = x_shift(rows, 1), x_shift(rows, -1)
    buf = put(put(buf, up, 3), down, 1)
    buf = put(buf, x_shift(up[:, :h], 1), 2)
    buf = put(buf, x_shift(down[:, h:], -1), 2, h)
    return buf.reshape(256, n)


def relative(rows, y, c):
    m = rows.shape[0]
    parts = rows.reshape(m, 2, NZ, 2, ROWS).transpose(1, 3, 0, 2, 4).reshape(2, 2, m, NZ * ROWS)
    parts = jnp.where(y == 0, parts, parts[::-1])
    parts = jnp.where(c == 0, parts, parts[:, ::-1])
    return parts.transpose(2, 0, 1, 3).reshape(m, 4 * NZ * ROWS)


def per_device(
    tokens,
    target,
    segment_ids,
    norm_gain,
    w_gate,
    w_up,
    w_down,
    dir_gate,
    dir_up,
    dir_down,
    ema_gate,
    ema_up,
    ema_down,
):
    s = lax.axis_index("seq")
    t = lax.axis_index("tensor")
    yh, z, c = s // 16, (s // 2) % 8, s % 2
    yl, x = t // 4, t % 4

    sign = 1 - 2 * c
    labels = jnp.arange(32, dtype=jnp.int32)
    onehot = (segment_ids[:, None] == labels[None, :]).astype(F32)

    own_in = jnp.concatenate([w_gate, w_up, dir_gate, dir_up], axis=1)
    tally = jnp.pad(jnp.sum(onehot, axis=0).astype(BF)[None], ((0, ROWS - 1), (0, TALLY - 32)))
    own_out = jnp.concatenate([w_down.T, dir_down.T, tally], axis=1)
    across_in = seq_swap(own_in, 16)
    near = gather_ring(own_in, z, sign)
    outs = group_gather(jnp.stack([own_out, seq_swap(own_out, 16)]), "seq", Z_GROUPS)
    near_other = seq_swap(near, 1)
    away = gather_ring(across_in, z, sign)
    outs_other = seq_swap(outs, 1)
    away_other = seq_swap(away, 1)

    wide = tokens.astype(F32)
    scale = lax.rsqrt(jnp.mean(wide * wide, axis=1, keepdims=True) + norm_eps)
    normed = (wide * scale * norm_gain).astype(BF)
    normed = relative(normed, yh, c)

    half = 2 * NZ * ROWS
    near_all = jnp.stack([near, near_other]).reshape(half, 4 * UNITS)
    away_all = jnp.stack([away, away_other]).reshape(half, 4 * UNITS)
    pre = product(normed[:, :half], near_all) + product(normed[:, half:], away_all)
    gate, upper, gate_dot, upper_dot = (pre[:, i * UNITS : (i + 1) * UNITS] for i in range(4))
    value, first, second = gelu_parts(gate)
    hidden = (value * upper).astype(BF)
    hidden_dot = (first * gate_dot * upper + value * upper_dot).astype(BF)

    outs_all = jnp.stack([outs, outs_other]).transpose(2, 0, 1, 3, 4)
    counts = jnp.sum(outs_all[:, :, :, 0, 2 * UNITS : 2 * UNITS + 32].astype(F32), axis=(0, 1, 2))
    down_all = outs_all[..., : 2 * UNITS].reshape(4 * NZ * ROWS, 2 * UNITS)
    mixed_part = against(hidden, down_all[:, :UNITS]).astype(BF)
    mixed_dot_part = against(jnp.concatenate([hidden_dot, hidden], axis=1), down_all).astype(BF)
    mixed = scatter_tensor(mixed_part, x, yl)
    mixed_dot = scatter_tensor(mixed_dot_part, x, yl)

    at = x * 64 + yl * 16
    my_tokens = relative(lax.dynamic_slice_in_dim(tokens, at, 16, 0), yh, c).astype(F32)
    my_target = relative(lax.dynamic_slice_in_dim(target, at, 16, 0), yh, c).astype(F32)
    my_hot = lax.dynamic_slice_in_dim(onehot, at, 16, 0)
    lengths = jnp.sum(my_hot * counts[None], axis=1, keepdims=True)
    my_grad = ((my_tokens + mixed - my_target) / lengths).astype(BF)
    my_grad_dot = (mixed_dot / lengths).astype(BF)
    grad_out = gather_tensor(my_grad, x, yl)
    grad_out_dot = gather_tensor(my_grad_dot, x, yl)

    back = product(grad_out, down_all)
    back_dot = product(grad_out_dot, down_all[:, :UNITS])
    grad_hidden = back[:, :UNITS]
    grad_hidden_dot = back_dot + back[:, UNITS:]
    grad_gate_dot = (
        (grad_hidden_dot * upper + grad_hidden * upper_dot) * first
        + grad_hidden * upper * second * gate_dot
    ).astype(BF)
    grad_upper_dot = (grad_hidden_dot * value + grad_hidden * first * gate_dot).astype(BF)
    grads = jnp.concatenate([grad_gate_dot, grad_upper_dot], axis=1)

    def terms(lo):
        rows = slice(lo, lo + half)
        part_in = over_tokens(normed[:, rows], grads).astype(BF)
        part_out = (
            over_tokens(grad_out[:, rows], hidden_dot) + over_tokens(grad_out_dot[:, rows], hidden)
        ).astype(BF)
        part = jnp.concatenate([part_in, part_out], axis=1).reshape(2, NZ, ROWS, 3 * UNITS)
        return (part[0].astype(F32) + seq_swap(part[1], 1).astype(F32)).astype(BF)

    away_terms = terms(half)
    near_terms = terms(0)
    near_tail = group_scatter(near_terms[..., UNITS:], "seq", Z_GROUPS).astype(F32)
    away_sum = exchange_sum(away_terms, "seq", Z_GROUPS).astype(BF)
    away_sum, head_terms = lax.optimization_barrier((away_sum, near_terms[..., :UNITS]))
    near_head = exchange_sum(head_terms, "seq", Z_GROUPS)
    away_sum = seq_swap(away_sum, 16).astype(F32)
    hvp = jnp.concatenate([near_head, near_tail], axis=1) + away_sum
    return (
        blend(ema_gate, dir_gate, hvp[:, :UNITS]),
        blend(ema_up, dir_up, hvp[:, UNITS : 2 * UNITS]),
        blend(ema_down, dir_down, hvp[:, 2 * UNITS :].T),
    )


def solution(mesh):
    in_specs = (
        P("seq", None),
        P("seq", None),
        P("seq"),
        P(),
        P("seq", "tensor"),
        P("seq", "tensor"),
        P("tensor", "seq"),
        P("seq", "tensor"),
        P("seq", "tensor"),
        P("tensor", "seq"),
        P("seq", "tensor"),
        P("seq", "tensor"),
        P("tensor", "seq"),
    )
    out_specs = (P("seq", "tensor"), P("seq", "tensor"), P("tensor", "seq"))
    return jax.shard_map(
        per_device, mesh=mesh, in_specs=in_specs, out_specs=out_specs, check_vma=False
    )
```

```python
import jax
import jax.numpy as jnp
from jax import lax
from jax.sharding import PartitionSpec as P

gelu_rate = 0.7978845608028654
gelu_cubic = 0.044715
beta_decay = 0.9
norm_eps = 1e-06

NZ = 8
ROWS = 72
UNITS = 288
TALLY = 64
BF = jnp.bfloat16
F32 = jnp.float32


def gelu_parts(pre):
    inner = gelu_rate * (pre + gelu_cubic * pre * pre * pre)
    slope = gelu_rate * (1.0 + 3.0 * gelu_cubic * pre * pre)
    bend = 6.0 * gelu_rate * gelu_cubic * pre
    tanh_val = jnp.tanh(inner)
    sech_sq = 1.0 - tanh_val * tanh_val
    value = 0.5 * pre * (1.0 + tanh_val)
    first = 0.5 * (1.0 + tanh_val) + 0.5 * pre * sech_sq * slope
    second = sech_sq * (slope + 0.5 * pre * (bend - 2.0 * tanh_val * slope * slope))
    return (value, first, second)


def product(left, right):
    return jnp.dot(left, right, preferred_element_type=F32)


def against(left, right):
    return lax.dot_general(left, right, (((1,), (1,)), ((), ())), preferred_element_type=F32)


def over_tokens(left, right):
    return lax.dot_general(left, right, (((0,), (0,)), ((), ())), preferred_element_type=F32)


def blend(ema, probe, hvp):
    return beta_decay * ema + (1.0 - beta_decay) * (probe.astype(F32) * hvp)


def ring_step(array):
    perm = [
        (s, (s // 16) * 16 + ((s // 2 % 8 + (1 - 2 * (s % 2))) % 8) * 2 + s % 2) for s in range(32)
    ]
    return lax.ppermute(array, "seq", perm)


def seq_swap(array, bit):
    return lax.ppermute(array, "seq", [(s, s ^ bit) for s in range(32)])


def y_swap(array, bit):
    return lax.ppermute(array, "tensor", [(t, t ^ (bit * 4)) for t in range(16)])


Z_GROUPS = [[y * 16 + z * 2 + c for z in range(8)] for y in range(2) for c in range(2)]
X_GROUPS = [[y * 4 + x for x in range(4)] for y in range(4)]
Y_GROUPS = [[y * 4 + x for y in range(4)] for x in range(4)]


def group_gather(array, axis, groups):
    return lax.all_gather(array, axis, axis_index_groups=groups)


def group_scatter(array, axis, groups):
    return lax.psum_scatter(array, axis, scatter_dimension=0, axis_index_groups=groups)


def group_exchange(array, axis, groups):
    return lax.all_to_all(array, axis, 0, 0, axis_index_groups=groups)


def gather_ring(chunk, z, sign):
    own = jnp.zeros((NZ,) + chunk.shape, chunk.dtype)
    held = chunk
    for k in range(NZ):
        own = lax.dynamic_update_slice(own, held[None], ((z - sign * k) % NZ, 0, 0))
        held = ring_step(held) if k < NZ - 1 else None
    return own


def exchange_sum(parts, axis, groups):
    return jnp.sum(group_exchange(parts, axis, groups).astype(F32), axis=0)


def x_step(array, by):
    perm = [
        (s * 16 + t, s * 16 + (t // 4) * 4 + (t % 4 + by * (1 - 2 * (s % 2))) % 4)
        for s in range(32)
        for t in range(16)
    ]
    return lax.ppermute(array, ("seq", "tensor"), perm)


def scatter_tensor(part, x, y, sign):
    n = part.shape[1]
    h = n // 2
    part = part.reshape(4, 64, n)

    def block(at):
        return lax.dynamic_index_in_dim(part, (x + sign * at) % 4, 0, keepdims=False)

    def add(left, right):
        return (left.astype(F32) + right.astype(F32)).astype(BF)

    far, ahead, behind = block(2), block(1), block(3)
    up, down = x_step(far[:, :h], 1), x_step(far[:, h:], -1)
    up = x_step(jnp.concatenate([add(ahead[:, :h], up), ahead[:, h:]], axis=1), 1)
    down = x_step(jnp.concatenate([behind[:, :h], add(behind[:, h:], down)], axis=1), -1)
    total = block(0).astype(F32) + up.astype(F32) + down.astype(F32)
    total = total.reshape(2, 2, 16, n)
    low = y % 2
    mine = lax.dynamic_index_in_dim(total, low, 1, keepdims=False)
    other = lax.dynamic_index_in_dim(total, 1 - low, 1, keepdims=False).astype(BF)
    mine = mine + y_swap(other, 1).astype(F32)
    high = y // 2
    own = lax.dynamic_index_in_dim(mine, high, 0, keepdims=False)
    other = lax.dynamic_index_in_dim(mine, 1 - high, 0, keepdims=False).astype(BF)
    return own + y_swap(other, 2).astype(F32)


def gather_tensor(own, x, y, sign):
    n = own.shape[1]
    h = n // 2
    low, high = y % 2, y // 2
    other = y_swap(own, 2)
    pair = jnp.where(high == 0, jnp.stack([own, other]), jnp.stack([other, own]))
    other = y_swap(pair, 1)
    rows = jnp.where(low == 0, jnp.stack([pair, other], axis=1), jnp.stack([other, pair], axis=1))
    rows = rows.reshape(64, n)
    buf = jnp.zeros((4, 64, n), own.dtype)

    def put(buf, piece, at, col=0):
        return lax.dynamic_update_slice(buf, piece[None], ((x + sign * at) % 4, 0, col))

    buf = put(buf, rows, 0)
    up, down = x_step(rows, 1), x_step(rows, -1)
    buf = put(put(buf, up, 3), down, 1)
    buf = put(buf, x_step(up[:, :h], 1), 2)
    buf = put(buf, x_step(down[:, h:], -1), 2, h)
    return buf.reshape(256, n)


def relative(rows, y):
    half = rows.shape[1] // 2
    low, high = rows[:, :half], rows[:, half:]
    return jnp.concatenate([jnp.where(y == 0, low, high), jnp.where(y == 0, high, low)], axis=1)


def interleave(mine, other, c, axis):
    first, second = jnp.where(c == 0, mine, other), jnp.where(c == 0, other, mine)
    return jnp.stack([first, second], axis=axis)


def per_device(
    tokens,
    target,
    segment_ids,
    norm_gain,
    w_gate,
    w_up,
    w_down,
    dir_gate,
    dir_up,
    dir_down,
    ema_gate,
    ema_up,
    ema_down,
):
    s = lax.axis_index("seq")
    t = lax.axis_index("tensor")
    yh, z, c = s // 16, (s // 2) % 8, s % 2
    yl, x = t // 4, t % 4

    sign = 1 - 2 * c
    labels = jnp.arange(32, dtype=jnp.int32)
    onehot = (segment_ids[:, None] == labels[None, :]).astype(F32)

    own_in = jnp.concatenate([w_gate, w_up, dir_gate, dir_up], axis=1)
    tally = jnp.pad(jnp.sum(onehot, axis=0).astype(BF)[None], ((0, ROWS - 1), (0, TALLY - 32)))
    own_out = jnp.concatenate([w_down.T, dir_down.T, tally], axis=1)
    across_in = seq_swap(own_in, 16)
    near = gather_ring(own_in, z, sign)
    outs = group_gather(jnp.stack([own_out, seq_swap(own_out, 16)]), "seq", Z_GROUPS)
    near_other = seq_swap(near, 1)
    away = gather_ring(across_in, z, sign)
    outs_other = seq_swap(outs, 1)
    away_other = seq_swap(away, 1)

    wide = tokens.astype(F32)
    scale = lax.rsqrt(jnp.mean(wide * wide, axis=1, keepdims=True) + norm_eps)
    normed = (wide * scale * norm_gain).astype(BF)
    normed = relative(normed, yh)

    half = 2 * NZ * ROWS
    near_all = interleave(near, near_other, c, 1).reshape(half, 4 * UNITS)
    away_all = interleave(away, away_other, c, 1).reshape(half, 4 * UNITS)
    pre = product(normed[:, :half], near_all) + product(normed[:, half:], away_all)
    gate, upper, gate_dot, upper_dot = (pre[:, i * UNITS : (i + 1) * UNITS] for i in range(4))
    value, first, second = gelu_parts(gate)
    hidden = (value * upper).astype(BF)
    hidden_dot = (first * gate_dot * upper + value * upper_dot).astype(BF)

    outs_all = interleave(outs, outs_other, c, 2).transpose(1, 0, 2, 3, 4)
    counts = jnp.sum(outs_all[:, :, :, 0, 2 * UNITS : 2 * UNITS + 32].astype(F32), axis=(0, 1, 2))
    down_all = outs_all[..., : 2 * UNITS].reshape(4 * NZ * ROWS, 2 * UNITS)
    mixed_part = against(hidden, down_all[:, :UNITS]).astype(BF)
    mixed_dot_part = against(jnp.concatenate([hidden_dot, hidden], axis=1), down_all).astype(BF)
    mixed = scatter_tensor(mixed_part, x, yl, sign)
    mixed_dot = scatter_tensor(mixed_dot_part, x, yl, sign)

    at = x * 64 + yl * 16
    my_tokens = relative(lax.dynamic_slice_in_dim(tokens, at, 16, 0), yh).astype(F32)
    my_target = relative(lax.dynamic_slice_in_dim(target, at, 16, 0), yh).astype(F32)
    my_hot = lax.dynamic_slice_in_dim(onehot, at, 16, 0)
    lengths = jnp.sum(my_hot * counts[None], axis=1, keepdims=True)
    my_grad = ((my_tokens + mixed - my_target) / lengths).astype(BF)
    my_grad_dot = (mixed_dot / lengths).astype(BF)
    grad_out = gather_tensor(my_grad, x, yl, sign)
    grad_out_dot = gather_tensor(my_grad_dot, x, yl, sign)

    back = product(grad_out, down_all)
    back_dot = product(grad_out_dot, down_all[:, :UNITS])
    grad_hidden = back[:, :UNITS]
    grad_hidden_dot = back_dot + back[:, UNITS:]
    grad_gate_dot = (
        (grad_hidden_dot * upper + grad_hidden * upper_dot) * first
        + grad_hidden * upper * second * gate_dot
    ).astype(BF)
    grad_upper_dot = (grad_hidden_dot * value + grad_hidden * first * gate_dot).astype(BF)
    grads = jnp.concatenate([grad_gate_dot, grad_upper_dot], axis=1)

    def terms(lo):
        rows = slice(lo, lo + half)
        part_in = over_tokens(normed[:, rows], grads).astype(BF)
        part_out = (
            over_tokens(grad_out[:, rows], hidden_dot) + over_tokens(grad_out_dot[:, rows], hidden)
        ).astype(BF)
        part = jnp.concatenate([part_in, part_out], axis=1).reshape(NZ, 2, ROWS, 3 * UNITS)
        mine = lax.dynamic_index_in_dim(part, c, 1, keepdims=False)
        other = lax.dynamic_index_in_dim(part, 1 - c, 1, keepdims=False)
        return (mine.astype(F32) + seq_swap(other, 1).astype(F32)).astype(BF)

    near_terms = terms(0)
    near_tail = group_scatter(near_terms[..., UNITS:], "seq", Z_GROUPS).astype(F32)
    away_terms = terms(half)
    sums = exchange_sum(
        jnp.concatenate([away_terms, near_terms[..., :UNITS]], axis=2), "seq", Z_GROUPS
    )
    away_sum = seq_swap(sums[:, : 3 * UNITS].astype(BF), 16).astype(F32)
    hvp = jnp.concatenate([sums[:, 3 * UNITS :], near_tail], axis=1) + away_sum
    return (
        blend(ema_gate, dir_gate, hvp[:, :UNITS]),
        blend(ema_up, dir_up, hvp[:, UNITS : 2 * UNITS]),
        blend(ema_down, dir_down, hvp[:, 2 * UNITS :].T),
    )


def solution(mesh):
    in_specs = (
        P("seq", None),
        P("seq", None),
        P("seq"),
        P(),
        P("seq", "tensor"),
        P("seq", "tensor"),
        P("tensor", "seq"),
        P("seq", "tensor"),
        P("seq", "tensor"),
        P("tensor", "seq"),
        P("seq", "tensor"),
        P("seq", "tensor"),
        P("tensor", "seq"),
    )
    out_specs = (P("seq", "tensor"), P("seq", "tensor"), P("tensor", "seq"))
    return jax.shard_map(
        per_device, mesh=mesh, in_specs=in_specs, out_specs=out_specs, check_vma=False
    )
```

```python
import jax
import jax.numpy as jnp
from jax import lax
from jax.sharding import PartitionSpec as P

gelu_rate = 0.7978845608028654
gelu_cubic = 0.044715
beta_decay = 0.9
norm_eps = 1e-06

NZ = 8
ROWS = 72
UNITS = 288
TALLY = 64
BF = jnp.bfloat16
F32 = jnp.float32


def gelu_parts(pre):
    inner = gelu_rate * (pre + gelu_cubic * pre * pre * pre)
    slope = gelu_rate * (1.0 + 3.0 * gelu_cubic * pre * pre)
    bend = 6.0 * gelu_rate * gelu_cubic * pre
    tanh_val = jnp.tanh(inner)
    sech_sq = 1.0 - tanh_val * tanh_val
    value = 0.5 * pre * (1.0 + tanh_val)
    first = 0.5 * (1.0 + tanh_val) + 0.5 * pre * sech_sq * slope
    second = sech_sq * (slope + 0.5 * pre * (bend - 2.0 * tanh_val * slope * slope))
    return (value, first, second)


def product(left, right):
    return jnp.dot(left, right, preferred_element_type=F32)


def against(left, right):
    return lax.dot_general(left, right, (((1,), (1,)), ((), ())), preferred_element_type=F32)


def over_tokens(left, right):
    return lax.dot_general(left, right, (((0,), (0,)), ((), ())), preferred_element_type=F32)


def blend(ema, probe, hvp):
    return beta_decay * ema + (1.0 - beta_decay) * (probe.astype(F32) * hvp)


def ring_step(array):
    perm = [
        (s, (s // 16) * 16 + ((s // 2 % 8 + (1 - 2 * (s % 2))) % 8) * 2 + s % 2) for s in range(32)
    ]
    return lax.ppermute(array, "seq", perm)


def seq_swap(array, bit):
    return lax.ppermute(array, "seq", [(s, s ^ bit) for s in range(32)])


def y_swap(array, bit):
    return lax.ppermute(array, "tensor", [(t, t ^ (bit * 4)) for t in range(16)])


Z_GROUPS = [[y * 16 + z * 2 + c for z in range(8)] for y in range(2) for c in range(2)]
X_GROUPS = [[y * 4 + x for x in range(4)] for y in range(4)]
Y_GROUPS = [[y * 4 + x for y in range(4)] for x in range(4)]


def group_gather(array, axis, groups):
    return lax.all_gather(array, axis, axis_index_groups=groups)


def group_scatter(array, axis, groups):
    return lax.psum_scatter(array, axis, scatter_dimension=0, axis_index_groups=groups)


def group_exchange(array, axis, groups):
    return lax.all_to_all(array, axis, 0, 0, axis_index_groups=groups)


def after(array, *earlier):
    for other in earlier:
        array = array + 0 * other[(slice(0, 1),) * other.ndim].reshape((1,) * array.ndim)
    return array


def ring_chunks(chunk, waits):
    held = [chunk]
    for k in range(1, NZ):
        held.append(ring_step(after(held[-1], *waits.get(k, ()))))
    return held


def in_order(held, z, sign):
    own = jnp.zeros((NZ,) + held[0].shape, held[0].dtype)
    for k, chunk in enumerate(held):
        own = lax.dynamic_update_slice(own, chunk[None], ((z - sign * k) % NZ, 0, 0))
    return own


def exchange_sum(parts, axis, groups):
    return jnp.sum(group_exchange(parts, axis, groups).astype(F32), axis=0)


def x_step(array, by):
    perm = [
        (s * 16 + t, s * 16 + (t // 4) * 4 + (t % 4 + by * (1 - 2 * (s % 2))) % 4)
        for s in range(32)
        for t in range(16)
    ]
    return lax.ppermute(array, ("seq", "tensor"), perm)


def scatter_tensor(part, x, y, sign):
    n = part.shape[1]
    h = n // 2
    part = part.reshape(4, 64, n)

    def block(at):
        return lax.dynamic_index_in_dim(part, (x + sign * at) % 4, 0, keepdims=False)

    def add(left, right):
        return (left.astype(F32) + right.astype(F32)).astype(BF)

    far, ahead, behind = block(2), block(1), block(3)
    up, down = x_step(far[:, :h], 1), x_step(far[:, h:], -1)
    up = x_step(jnp.concatenate([add(ahead[:, :h], up), ahead[:, h:]], axis=1), 1)
    down = x_step(jnp.concatenate([behind[:, :h], add(behind[:, h:], down)], axis=1), -1)
    total = block(0).astype(F32) + up.astype(F32) + down.astype(F32)
    total = total.reshape(2, 2, 16, n)
    low = y % 2
    mine = lax.dynamic_index_in_dim(total, low, 1, keepdims=False)
    other = lax.dynamic_index_in_dim(total, 1 - low, 1, keepdims=False).astype(BF)
    mine = mine + y_swap(other, 1).astype(F32)
    high = y // 2
    own = lax.dynamic_index_in_dim(mine, high, 0, keepdims=False)
    other = lax.dynamic_index_in_dim(mine, 1 - high, 0, keepdims=False).astype(BF)
    return own + y_swap(other, 2).astype(F32)


def gather_tensor(own, x, y, sign):
    n = own.shape[1]
    h = n // 2
    low, high = y % 2, y // 2
    other = y_swap(own, 2)
    pair = jnp.where(high == 0, jnp.stack([own, other]), jnp.stack([other, own]))
    other = y_swap(pair, 1)
    rows = jnp.where(low == 0, jnp.stack([pair, other], axis=1), jnp.stack([other, pair], axis=1))
    rows = rows.reshape(64, n)
    buf = jnp.zeros((4, 64, n), own.dtype)

    def put(buf, piece, at, col=0):
        return lax.dynamic_update_slice(buf, piece[None], ((x + sign * at) % 4, 0, col))

    buf = put(buf, rows, 0)
    up, down = x_step(rows, 1), x_step(rows, -1)
    buf = put(put(buf, up, 3), down, 1)
    buf = put(buf, x_step(up[:, :h], 1), 2)
    buf = put(buf, x_step(down[:, h:], -1), 2, h)
    return buf.reshape(256, n)


def relative(rows, y):
    half = rows.shape[1] // 2
    low, high = rows[:, :half], rows[:, half:]
    return jnp.concatenate([jnp.where(y == 0, low, high), jnp.where(y == 0, high, low)], axis=1)


def interleave(mine, other, c, axis):
    first, second = jnp.where(c == 0, mine, other), jnp.where(c == 0, other, mine)
    return jnp.stack([first, second], axis=axis)


def per_device(
    tokens,
    target,
    segment_ids,
    norm_gain,
    w_gate,
    w_up,
    w_down,
    dir_gate,
    dir_up,
    dir_down,
    ema_gate,
    ema_up,
    ema_down,
):
    s = lax.axis_index("seq")
    t = lax.axis_index("tensor")
    yh, z, c = s // 16, (s // 2) % 8, s % 2
    yl, x = t // 4, t % 4

    sign = 1 - 2 * c
    labels = jnp.arange(32, dtype=jnp.int32)
    onehot = (segment_ids[:, None] == labels[None, :]).astype(F32)

    own_in = jnp.concatenate([w_gate, w_up, dir_gate, dir_up], axis=1)
    tally = jnp.pad(jnp.sum(onehot, axis=0).astype(BF)[None], ((0, ROWS - 1), (0, TALLY - 32)))
    own_out = jnp.concatenate([w_down.T, dir_down.T, tally], axis=1)
    across_in = seq_swap(own_in, 16)
    near_held = ring_chunks(own_in, {})
    own_out = after(own_out, near_held[1])
    outs = group_gather(jnp.stack([own_out, seq_swap(own_out, 16)]), "seq", Z_GROUPS)
    outs_other = seq_swap(outs, 1)
    near = in_order(near_held, z, sign)
    near_other = seq_swap(near, 1)
    away = in_order(ring_chunks(across_in, {1: (near_held[2],), 7: (outs_other,)}), z, sign)
    away_other = seq_swap(away, 1)

    wide = tokens.astype(F32)
    scale = lax.rsqrt(jnp.mean(wide * wide, axis=1, keepdims=True) + norm_eps)
    normed = (wide * scale * norm_gain).astype(BF)
    normed = relative(normed, yh)

    half = 2 * NZ * ROWS
    near_all = interleave(near, near_other, c, 1).reshape(half, 4 * UNITS)
    away_all = interleave(away, away_other, c, 1).reshape(half, 4 * UNITS)
    pre = product(normed[:, :half], near_all) + product(normed[:, half:], away_all)
    gate, upper, gate_dot, upper_dot = (pre[:, i * UNITS : (i + 1) * UNITS] for i in range(4))
    value, first, second = gelu_parts(gate)
    hidden = (value * upper).astype(BF)
    hidden_dot = (first * gate_dot * upper + value * upper_dot).astype(BF)

    outs_all = interleave(outs, outs_other, c, 2).transpose(1, 0, 2, 3, 4)
    counts = jnp.sum(outs_all[:, :, :, 0, 2 * UNITS : 2 * UNITS + 32].astype(F32), axis=(0, 1, 2))
    down_all = outs_all[..., : 2 * UNITS].reshape(4 * NZ * ROWS, 2 * UNITS)
    mixed_part = against(hidden, down_all[:, :UNITS]).astype(BF)
    mixed_dot_part = against(jnp.concatenate([hidden_dot, hidden], axis=1), down_all).astype(BF)
    mixed = scatter_tensor(mixed_part, x, yl, sign)
    mixed_dot = scatter_tensor(mixed_dot_part, x, yl, sign)

    at = x * 64 + yl * 16
    my_tokens = relative(lax.dynamic_slice_in_dim(tokens, at, 16, 0), yh).astype(F32)
    my_target = relative(lax.dynamic_slice_in_dim(target, at, 16, 0), yh).astype(F32)
    my_hot = lax.dynamic_slice_in_dim(onehot, at, 16, 0)
    lengths = jnp.sum(my_hot * counts[None], axis=1, keepdims=True)
    my_grad = ((my_tokens + mixed - my_target) / lengths).astype(BF)
    my_grad_dot = (mixed_dot / lengths).astype(BF)
    grad_out = gather_tensor(my_grad, x, yl, sign)
    grad_out_dot = gather_tensor(my_grad_dot, x, yl, sign)

    back = product(grad_out, down_all)
    back_dot = product(grad_out_dot, down_all[:, :UNITS])
    grad_hidden = back[:, :UNITS]
    grad_hidden_dot = back_dot + back[:, UNITS:]
    grad_gate_dot = (
        (grad_hidden_dot * upper + grad_hidden * upper_dot) * first
        + grad_hidden * upper * second * gate_dot
    ).astype(BF)
    grad_upper_dot = (grad_hidden_dot * value + grad_hidden * first * gate_dot).astype(BF)
    grads = jnp.concatenate([grad_gate_dot, grad_upper_dot], axis=1)

    part_in = over_tokens(normed, grads).astype(BF)
    part_out = (over_tokens(grad_out, hidden_dot) + over_tokens(grad_out_dot, hidden)).astype(BF)
    part = jnp.concatenate([part_in, part_out], axis=1).reshape(2, NZ, 2, ROWS, 3 * UNITS)
    mine = jnp.where(c == 0, part[:, :, 0], part[:, :, 1])
    other = jnp.where(c == 0, part[:, :, 1], part[:, :, 0])
    near_terms, away_terms = (mine.astype(F32) + seq_swap(other, 1).astype(F32)).astype(BF)
    near_tail = group_scatter(near_terms[..., UNITS:], "seq", Z_GROUPS).astype(F32)
    sums = exchange_sum(
        jnp.concatenate([away_terms, near_terms[..., :UNITS]], axis=2), "seq", Z_GROUPS
    )
    away_sum = seq_swap(sums[:, : 3 * UNITS].astype(BF), 16).astype(F32)
    hvp = jnp.concatenate([sums[:, 3 * UNITS :], near_tail], axis=1) + away_sum
    return (
        blend(ema_gate, dir_gate, hvp[:, :UNITS]),
        blend(ema_up, dir_up, hvp[:, UNITS : 2 * UNITS]),
        blend(ema_down, dir_down, hvp[:, 2 * UNITS :].T),
    )


def solution(mesh):
    in_specs = (
        P("seq", None),
        P("seq", None),
        P("seq"),
        P(),
        P("seq", "tensor"),
        P("seq", "tensor"),
        P("tensor", "seq"),
        P("seq", "tensor"),
        P("seq", "tensor"),
        P("tensor", "seq"),
        P("seq", "tensor"),
        P("seq", "tensor"),
        P("tensor", "seq"),
    )
    out_specs = (P("seq", "tensor"), P("seq", "tensor"), P("tensor", "seq"))
    return jax.shard_map(
        per_device, mesh=mesh, in_specs=in_specs, out_specs=out_specs, check_vma=False
    )
```

```python
import jax
import jax.numpy as jnp
from jax import lax
from jax.sharding import PartitionSpec as P

gelu_rate = 0.7978845608028654
gelu_cubic = 0.044715
beta_decay = 0.9
norm_eps = 1e-06

NZ = 8
ROWS = 72
UNITS = 288
TALLY = 64
BF = jnp.bfloat16
F32 = jnp.float32


def gelu_parts(pre):
    inner = gelu_rate * (pre + gelu_cubic * pre * pre * pre)
    slope = gelu_rate * (1.0 + 3.0 * gelu_cubic * pre * pre)
    bend = 6.0 * gelu_rate * gelu_cubic * pre
    tanh_val = jnp.tanh(inner)
    sech_sq = 1.0 - tanh_val * tanh_val
    value = 0.5 * pre * (1.0 + tanh_val)
    first = 0.5 * (1.0 + tanh_val) + 0.5 * pre * sech_sq * slope
    second = sech_sq * (slope + 0.5 * pre * (bend - 2.0 * tanh_val * slope * slope))
    return (value, first, second)


def product(left, right):
    return jnp.dot(left, right, preferred_element_type=F32)


def against(left, right):
    return lax.dot_general(left, right, (((1,), (1,)), ((), ())), preferred_element_type=F32)


def over_tokens(left, right):
    return lax.dot_general(left, right, (((0,), (0,)), ((), ())), preferred_element_type=F32)


def blend(ema, probe, hvp):
    return beta_decay * ema + (1.0 - beta_decay) * (probe.astype(F32) * hvp)


def ring_step(array):
    perm = [
        (s, (s // 16) * 16 + ((s // 2 % 8 + (1 - 2 * (s % 2))) % 8) * 2 + s % 2) for s in range(32)
    ]
    return lax.ppermute(array, "seq", perm)


def seq_swap(array, bit):
    return lax.ppermute(array, "seq", [(s, s ^ bit) for s in range(32)])


def y_swap(array, bit):
    return lax.ppermute(array, "tensor", [(t, t ^ (bit * 4)) for t in range(16)])


Z_GROUPS = [[y * 16 + z * 2 + c for z in range(8)] for y in range(2) for c in range(2)]
X_GROUPS = [[y * 4 + x for x in range(4)] for y in range(4)]
Y_GROUPS = [[y * 4 + x for y in range(4)] for x in range(4)]


def group_gather(array, axis, groups):
    return lax.all_gather(array, axis, axis_index_groups=groups)


def group_scatter(array, axis, groups):
    return lax.psum_scatter(array, axis, scatter_dimension=0, axis_index_groups=groups)


def group_exchange(array, axis, groups):
    return lax.all_to_all(array, axis, 0, 0, axis_index_groups=groups)


def after(array, *earlier):
    for other in earlier:
        array = array + 0 * other[(slice(0, 1),) * other.ndim].reshape((1,) * array.ndim)
    return array


def ring_chunks(chunk):
    held = [chunk]
    for k in range(1, NZ):
        held.append(ring_step(held[-1]))
    return held


def in_order(held, z, sign):
    own = jnp.zeros((NZ,) + held[0].shape, held[0].dtype)
    for k, chunk in enumerate(held):
        own = lax.dynamic_update_slice(own, chunk[None], ((z - sign * k) % NZ, 0, 0))
    return own


def exchange_sum(parts, axis, groups):
    return jnp.sum(group_exchange(parts, axis, groups).astype(F32), axis=0)


def x_shift(array, by):
    perm = [(t, (t // 4) * 4 + (t % 4 + by) % 4) for t in range(16)]
    return lax.ppermute(array, "tensor", perm)


def scatter_tensor(parts, x, y):
    n = parts[0].shape[1]
    h = n // 2
    parts = [part.reshape(4, 64, n) for part in parts]

    def block(part, at):
        return lax.dynamic_index_in_dim(part, (x + at) % 4, 0, keepdims=False)

    def add(left, right):
        return (left.astype(F32) + right.astype(F32)).astype(BF)

    def onward(part, up, down):
        ahead, behind = block(part, 1), block(part, 3)
        return (
            jnp.concatenate([add(ahead[:, :h], up), ahead[:, h:]], axis=1),
            jnp.concatenate([behind[:, :h], add(behind[:, h:], down)], axis=1),
        )

    far = [block(part, 2) for part in parts]
    ups = [x_shift(f[:, :h], 1) for f in far]
    downs = [x_shift(f[:, h:], -1) for f in far]
    pairs = [onward(*each) for each in zip(parts, ups, downs)]
    ups = [x_shift(up, 1) for up, _ in pairs]
    downs = [x_shift(down, -1) for _, down in pairs]
    low, high = y % 2, y // 2
    sums = [
        (block(part, 0).astype(F32) + up.astype(F32) + down.astype(F32)).reshape(2, 2, 16, n)
        for part, up, down in zip(parts, ups, downs)
    ]
    sent = [lax.dynamic_index_in_dim(s, 1 - low, 1, keepdims=False).astype(BF) for s in sums]
    got = [y_swap(s, 1) for s in sent]
    sums = [
        lax.dynamic_index_in_dim(s, low, 1, keepdims=False) + g.astype(F32)
        for s, g in zip(sums, got)
    ]
    sent = [lax.dynamic_index_in_dim(s, 1 - high, 0, keepdims=False).astype(BF) for s in sums]
    got = [y_swap(s, 2) for s in sent]
    return [
        lax.dynamic_index_in_dim(s, high, 0, keepdims=False) + g.astype(F32)
        for s, g in zip(sums, got)
    ]


def gather_tensor(owns, x, y):
    n = owns[0].shape[1]
    h = n // 2
    low, high = y % 2, y // 2
    others = [y_swap(own, 2) for own in owns]
    pairs = [
        jnp.where(high == 0, jnp.stack([own, other]), jnp.stack([other, own]))
        for own, other in zip(owns, others)
    ]
    others = [y_swap(pair, 1) for pair in pairs]
    rows = [
        jnp.where(
            low == 0, jnp.stack([pair, other], axis=1), jnp.stack([other, pair], axis=1)
        ).reshape(64, n)
        for pair, other in zip(pairs, others)
    ]

    def put(buf, piece, at, col=0):
        return lax.dynamic_update_slice(buf, piece[None], ((x + at) % 4, 0, col))

    ups = [x_shift(r, 1) for r in rows]
    downs = [x_shift(r, -1) for r in rows]
    far_ups = [x_shift(up[:, :h], 1) for up in ups]
    far_downs = [x_shift(down[:, h:], -1) for down in downs]
    result = []
    for own, up, down, far_up, far_down in zip(rows, ups, downs, far_ups, far_downs):
        buf = put(jnp.zeros((4, 64, n), own.dtype), own, 0)
        buf = put(put(buf, up, 3), down, 1)
        buf = put(put(buf, far_up, 2), far_down, 2, h)
        result.append(buf.reshape(256, n))
    return result


def relative(rows, y, c):
    m = rows.shape[0]
    parts = rows.reshape(m, 2, NZ, 2, ROWS).transpose(1, 3, 0, 2, 4).reshape(2, 2, m, NZ * ROWS)
    parts = jnp.where(y == 0, parts, parts[::-1])
    parts = jnp.where(c == 0, parts, parts[:, ::-1])
    return parts.transpose(2, 0, 1, 3).reshape(m, 4 * NZ * ROWS)


def per_device(
    tokens,
    target,
    segment_ids,
    norm_gain,
    w_gate,
    w_up,
    w_down,
    dir_gate,
    dir_up,
    dir_down,
    ema_gate,
    ema_up,
    ema_down,
):
    s = lax.axis_index("seq")
    t = lax.axis_index("tensor")
    yh, z, c = s // 16, (s // 2) % 8, s % 2
    yl, x = t // 4, t % 4

    sign = 1 - 2 * c
    labels = jnp.arange(32, dtype=jnp.int32)
    onehot = (segment_ids[:, None] == labels[None, :]).astype(F32)

    own_in = jnp.concatenate([w_gate, w_up, dir_gate, dir_up], axis=1)
    tally = jnp.pad(jnp.sum(onehot, axis=0).astype(BF)[None], ((0, ROWS - 1), (0, TALLY - 32)))
    own_out = jnp.concatenate([w_down.T, dir_down.T, tally], axis=1)
    across_in = seq_swap(own_in, 16)
    near_held = ring_chunks(own_in)
    near = in_order(near_held, z, sign)
    own_out = after(own_out, near_held[1])
    outs = group_gather(jnp.stack([own_out, seq_swap(own_out, 16)]), "seq", Z_GROUPS)
    near_other = seq_swap(near, 1)
    away = in_order(ring_chunks(across_in), z, sign)
    outs_other = seq_swap(outs, 1)
    away_other = seq_swap(away, 1)

    tokens = after(tokens, near_held[-1])
    target = after(target, near_held[-1])
    wide = tokens.astype(F32)
    scale = lax.rsqrt(jnp.mean(wide * wide, axis=1, keepdims=True) + norm_eps)
    normed = (wide * scale * norm_gain).astype(BF)
    normed = relative(normed, yh, c)

    half = 2 * NZ * ROWS
    near_all = jnp.stack([near, near_other]).reshape(half, 4 * UNITS)
    away_all = jnp.stack([away, away_other]).reshape(half, 4 * UNITS)
    pre = product(normed[:, :half], near_all) + product(normed[:, half:], away_all)
    gate, upper, gate_dot, upper_dot = (pre[:, i * UNITS : (i + 1) * UNITS] for i in range(4))
    value, first, second = gelu_parts(gate)
    hidden = (value * upper).astype(BF)
    hidden_dot = (first * gate_dot * upper + value * upper_dot).astype(BF)

    outs_all = jnp.stack([outs, outs_other]).transpose(2, 0, 1, 3, 4)
    counts = jnp.sum(outs_all[:, :, :, 0, 2 * UNITS : 2 * UNITS + 32].astype(F32), axis=(0, 1, 2))
    down_all = outs_all[..., : 2 * UNITS].reshape(4 * NZ * ROWS, 2 * UNITS)
    mixed_part = against(hidden, down_all[:, :UNITS]).astype(BF)
    mixed_dot_part = against(jnp.concatenate([hidden_dot, hidden], axis=1), down_all).astype(BF)
    mixed, mixed_dot = scatter_tensor([mixed_part, mixed_dot_part], x, yl)

    at = x * 64 + yl * 16
    my_tokens = relative(lax.dynamic_slice_in_dim(tokens, at, 16, 0), yh, c).astype(F32)
    my_target = relative(lax.dynamic_slice_in_dim(target, at, 16, 0), yh, c).astype(F32)
    my_hot = lax.dynamic_slice_in_dim(onehot, at, 16, 0)
    lengths = jnp.sum(my_hot * counts[None], axis=1, keepdims=True)
    my_grad = ((my_tokens + mixed - my_target) / lengths).astype(BF)
    my_grad_dot = (mixed_dot / lengths).astype(BF)
    grad_out, grad_out_dot = gather_tensor([my_grad, my_grad_dot], x, yl)

    back = product(grad_out, down_all)
    back_dot = product(grad_out_dot, down_all[:, :UNITS])
    grad_hidden = back[:, :UNITS]
    grad_hidden_dot = back_dot + back[:, UNITS:]
    grad_gate_dot = (
        (grad_hidden_dot * upper + grad_hidden * upper_dot) * first
        + grad_hidden * upper * second * gate_dot
    ).astype(BF)
    grad_upper_dot = (grad_hidden_dot * value + grad_hidden * first * gate_dot).astype(BF)
    grads = jnp.concatenate([grad_gate_dot, grad_upper_dot], axis=1)

    def terms(lo):
        rows = slice(lo, lo + half)
        part_in = over_tokens(normed[:, rows], grads).astype(BF)
        part_out = (
            over_tokens(grad_out[:, rows], hidden_dot) + over_tokens(grad_out_dot[:, rows], hidden)
        ).astype(BF)
        part = jnp.concatenate([part_in, part_out], axis=1).reshape(2, NZ, ROWS, 3 * UNITS)
        return (part[0].astype(F32) + seq_swap(part[1], 1).astype(F32)).astype(BF)

    near_terms = terms(0)
    away_terms = terms(half)
    near_tail = group_scatter(near_terms[..., UNITS:], "seq", Z_GROUPS).astype(F32)
    sums = exchange_sum(
        jnp.concatenate([away_terms, near_terms[..., :UNITS]], axis=2), "seq", Z_GROUPS
    )
    away_sum = seq_swap(sums[:, : 3 * UNITS].astype(BF), 16).astype(F32)
    hvp = jnp.concatenate([sums[:, 3 * UNITS :], near_tail], axis=1) + away_sum
    return (
        blend(ema_gate, dir_gate, hvp[:, :UNITS]),
        blend(ema_up, dir_up, hvp[:, UNITS : 2 * UNITS]),
        blend(ema_down, dir_down, hvp[:, 2 * UNITS :].T),
    )


def solution(mesh):
    in_specs = (
        P("seq", None),
        P("seq", None),
        P("seq"),
        P(),
        P("seq", "tensor"),
        P("seq", "tensor"),
        P("tensor", "seq"),
        P("seq", "tensor"),
        P("seq", "tensor"),
        P("tensor", "seq"),
        P("seq", "tensor"),
        P("seq", "tensor"),
        P("tensor", "seq"),
    )
    out_specs = (P("seq", "tensor"), P("seq", "tensor"), P("tensor", "seq"))
    return jax.shard_map(
        per_device, mesh=mesh, in_specs=in_specs, out_specs=out_specs, check_vma=False
    )
```

```python
import jax
import jax.numpy as jnp
from jax import lax
from jax.sharding import PartitionSpec as P

gelu_rate = 0.7978845608028654
gelu_cubic = 0.044715
beta_decay = 0.9
norm_eps = 1e-06

NZ = 8
ROWS = 72
UNITS = 288
TALLY = 64
BF = jnp.bfloat16
F32 = jnp.float32


def gelu_parts(pre):
    inner = gelu_rate * (pre + gelu_cubic * pre * pre * pre)
    slope = gelu_rate * (1.0 + 3.0 * gelu_cubic * pre * pre)
    bend = 6.0 * gelu_rate * gelu_cubic * pre
    tanh_val = jnp.tanh(inner)
    sech_sq = 1.0 - tanh_val * tanh_val
    value = 0.5 * pre * (1.0 + tanh_val)
    first = 0.5 * (1.0 + tanh_val) + 0.5 * pre * sech_sq * slope
    second = sech_sq * (slope + 0.5 * pre * (bend - 2.0 * tanh_val * slope * slope))
    return (value, first, second)


def product(left, right):
    return jnp.dot(left, right, preferred_element_type=F32)


def against(left, right):
    return lax.dot_general(left, right, (((1,), (1,)), ((), ())), preferred_element_type=F32)


def over_tokens(left, right):
    return lax.dot_general(left, right, (((0,), (0,)), ((), ())), preferred_element_type=F32)


def blend(ema, probe, hvp):
    return beta_decay * ema + (1.0 - beta_decay) * (probe.astype(F32) * hvp)


def ring_step(array):
    perm = [
        (s, (s // 16) * 16 + ((s // 2 % 8 + (1 - 2 * (s % 2))) % 8) * 2 + s % 2) for s in range(32)
    ]
    return lax.ppermute(array, "seq", perm)


def seq_swap(array, bit):
    return lax.ppermute(array, "seq", [(s, s ^ bit) for s in range(32)])


def y_swap(array, bit):
    return lax.ppermute(array, "tensor", [(t, t ^ (bit * 4)) for t in range(16)])


Z_GROUPS = [[y * 16 + z * 2 + c for z in range(8)] for y in range(2) for c in range(2)]
X_GROUPS = [[y * 4 + x for x in range(4)] for y in range(4)]
Y_GROUPS = [[y * 4 + x for y in range(4)] for x in range(4)]


def group_gather(array, axis, groups):
    return lax.all_gather(array, axis, axis_index_groups=groups)


def group_scatter(array, axis, groups):
    return lax.psum_scatter(array, axis, scatter_dimension=0, axis_index_groups=groups)


def group_exchange(array, axis, groups):
    return lax.all_to_all(array, axis, 0, 0, axis_index_groups=groups)


def after(array, *earlier):
    for other in earlier:
        array = array + 0 * other[(slice(0, 1),) * other.ndim].reshape((1,) * array.ndim)
    return array


def ring_chunks(chunk):
    held = [chunk]
    for k in range(1, NZ):
        held.append(ring_step(held[-1]))
    return held


def in_order(held, z, sign):
    own = jnp.zeros((NZ,) + held[0].shape, held[0].dtype)
    for k, chunk in enumerate(held):
        own = lax.dynamic_update_slice(own, chunk[None], ((z - sign * k) % NZ, 0, 0))
    return own


def exchange_sum(parts, axis, groups):
    return jnp.sum(group_exchange(parts, axis, groups).astype(F32), axis=0)


def x_shift(array, by):
    perm = [(t, (t // 4) * 4 + (t % 4 + by) % 4) for t in range(16)]
    return lax.ppermute(array, "tensor", perm)


def scatter_tensor(parts, x, y):
    n = parts[0].shape[1]
    h = n // 2
    parts = [part.reshape(4, 64, n) for part in parts]

    def block(part, at):
        return lax.dynamic_index_in_dim(part, (x + at) % 4, 0, keepdims=False)

    def add(left, right):
        return (left.astype(F32) + right.astype(F32)).astype(BF)

    def onward(part, up, down):
        ahead, behind = block(part, 1), block(part, 3)
        return (
            jnp.concatenate([add(ahead[:, :h], up), ahead[:, h:]], axis=1),
            jnp.concatenate([behind[:, :h], add(behind[:, h:], down)], axis=1),
        )

    far = [block(part, 2) for part in parts]
    ups = [x_shift(f[:, :h], 1) for f in far]
    downs = [x_shift(f[:, h:], -1) for f in far]
    pairs = [onward(*each) for each in zip(parts, ups, downs)]
    ups = [x_shift(up, 1) for up, _ in pairs]
    downs = [x_shift(down, -1) for _, down in pairs]
    low, high = y % 2, y // 2
    sums = [
        (block(part, 0).astype(F32) + up.astype(F32) + down.astype(F32)).reshape(2, 2, 16, n)
        for part, up, down in zip(parts, ups, downs)
    ]
    sent = [lax.dynamic_index_in_dim(s, 1 - low, 1, keepdims=False).astype(BF) for s in sums]
    got = [y_swap(s, 1) for s in sent]
    sums = [
        lax.dynamic_index_in_dim(s, low, 1, keepdims=False) + g.astype(F32)
        for s, g in zip(sums, got)
    ]
    sent = [lax.dynamic_index_in_dim(s, 1 - high, 0, keepdims=False).astype(BF) for s in sums]
    got = [y_swap(s, 2) for s in sent]
    return [
        lax.dynamic_index_in_dim(s, high, 0, keepdims=False) + g.astype(F32)
        for s, g in zip(sums, got)
    ]


def gather_tensor(owns, x, y):
    n = owns[0].shape[1]
    h = n // 2
    low, high = y % 2, y // 2
    others = [y_swap(own, 2) for own in owns]
    pairs = [
        jnp.where(high == 0, jnp.stack([own, other]), jnp.stack([other, own]))
        for own, other in zip(owns, others)
    ]
    others = [y_swap(pair, 1) for pair in pairs]
    rows = [
        jnp.where(
            low == 0, jnp.stack([pair, other], axis=1), jnp.stack([other, pair], axis=1)
        ).reshape(64, n)
        for pair, other in zip(pairs, others)
    ]

    def put(buf, piece, at, col=0):
        return lax.dynamic_update_slice(buf, piece[None], ((x + at) % 4, 0, col))

    own = rows[0]
    up, down = x_shift(own, 1), x_shift(own, -1)
    second = group_gather(rows[1], "tensor", X_GROUPS)
    buf = put(jnp.zeros((4, 64, n), own.dtype), own, 0)
    buf = put(put(buf, up, 3), down, 1)
    buf = put(buf, x_shift(up[:, :h], 1), 2)
    buf = put(buf, x_shift(down[:, h:], -1), 2, h)
    return [buf.reshape(256, n), second.reshape(256, n)]


def relative(rows, y, c):
    m = rows.shape[0]
    parts = rows.reshape(m, 2, NZ, 2, ROWS).transpose(1, 3, 0, 2, 4).reshape(2, 2, m, NZ * ROWS)
    parts = jnp.where(y == 0, parts, parts[::-1])
    parts = jnp.where(c == 0, parts, parts[:, ::-1])
    return parts.transpose(2, 0, 1, 3).reshape(m, 4 * NZ * ROWS)


def per_device(
    tokens,
    target,
    segment_ids,
    norm_gain,
    w_gate,
    w_up,
    w_down,
    dir_gate,
    dir_up,
    dir_down,
    ema_gate,
    ema_up,
    ema_down,
):
    s = lax.axis_index("seq")
    t = lax.axis_index("tensor")
    yh, z, c = s // 16, (s // 2) % 8, s % 2
    yl, x = t // 4, t % 4

    sign = 1 - 2 * c
    labels = jnp.arange(32, dtype=jnp.int32)
    onehot = (segment_ids[:, None] == labels[None, :]).astype(F32)

    own_in = jnp.concatenate([w_gate, w_up, dir_gate, dir_up], axis=1)
    tally = jnp.pad(jnp.sum(onehot, axis=0).astype(BF)[None], ((0, ROWS - 1), (0, TALLY - 32)))
    own_out = jnp.concatenate([w_down.T, dir_down.T, tally], axis=1)
    across_in = seq_swap(own_in, 16)
    near = group_exchange(jnp.broadcast_to(own_in[None], (NZ,) + own_in.shape), "seq", Z_GROUPS)
    outs = group_gather(jnp.stack([own_out, seq_swap(own_out, 16)]), "seq", Z_GROUPS)
    away_held = ring_chunks(across_in)
    near_other = seq_swap(near, 1)
    outs_other = seq_swap(outs, 1)
    away = in_order(away_held, z, sign)
    away_other = seq_swap(away, 1)

    tokens = after(tokens, away_held[1])
    target = after(target, away_held[2])
    wide = tokens.astype(F32)
    scale = lax.rsqrt(jnp.mean(wide * wide, axis=1, keepdims=True) + norm_eps)
    normed = (wide * scale * norm_gain).astype(BF)
    normed = relative(normed, yh, c)

    half = 2 * NZ * ROWS
    near_all = jnp.stack([near, near_other]).reshape(half, 4 * UNITS)
    away_all = jnp.stack([away, away_other]).reshape(half, 4 * UNITS)
    pre = product(normed[:, :half], near_all) + product(normed[:, half:], away_all)
    gate, upper, gate_dot, upper_dot = (pre[:, i * UNITS : (i + 1) * UNITS] for i in range(4))
    value, first, second = gelu_parts(gate)
    hidden = (value * upper).astype(BF)
    hidden_dot = (first * gate_dot * upper + value * upper_dot).astype(BF)

    outs_all = jnp.stack([outs, outs_other]).transpose(2, 0, 1, 3, 4)
    counts = jnp.sum(outs_all[:, :, :, 0, 2 * UNITS : 2 * UNITS + 32].astype(F32), axis=(0, 1, 2))
    down_all = outs_all[..., : 2 * UNITS].reshape(4 * NZ * ROWS, 2 * UNITS)
    mixed_part = against(hidden, down_all[:, :UNITS]).astype(BF)
    mixed_dot_part = against(jnp.concatenate([hidden_dot, hidden], axis=1), down_all).astype(BF)
    mixed, mixed_dot = scatter_tensor([mixed_part, mixed_dot_part], x, yl)

    at = x * 64 + yl * 16
    my_tokens = relative(lax.dynamic_slice_in_dim(tokens, at, 16, 0), yh, c).astype(F32)
    my_target = relative(lax.dynamic_slice_in_dim(target, at, 16, 0), yh, c).astype(F32)
    my_hot = lax.dynamic_slice_in_dim(onehot, at, 16, 0)
    lengths = jnp.sum(my_hot * counts[None], axis=1, keepdims=True)
    my_grad = ((my_tokens + mixed - my_target) / lengths).astype(BF)
    my_grad_dot = (mixed_dot / lengths).astype(BF)
    grad_out, grad_out_dot = gather_tensor([my_grad, my_grad_dot], x, yl)

    back = product(grad_out, down_all)
    back_dot = product(grad_out_dot, down_all[:, :UNITS])
    grad_hidden = back[:, :UNITS]
    grad_hidden_dot = back_dot + back[:, UNITS:]
    grad_gate_dot = (
        (grad_hidden_dot * upper + grad_hidden * upper_dot) * first
        + grad_hidden * upper * second * gate_dot
    ).astype(BF)
    grad_upper_dot = (grad_hidden_dot * value + grad_hidden * first * gate_dot).astype(BF)
    grads = jnp.concatenate([grad_gate_dot, grad_upper_dot], axis=1)

    def terms(lo):
        rows = slice(lo, lo + half)
        part_in = over_tokens(normed[:, rows], grads).astype(BF)
        part_out = (
            over_tokens(grad_out[:, rows], hidden_dot) + over_tokens(grad_out_dot[:, rows], hidden)
        ).astype(BF)
        part = jnp.concatenate([part_in, part_out], axis=1).reshape(2, NZ, ROWS, 3 * UNITS)
        return (part[0].astype(F32) + seq_swap(part[1], 1).astype(F32)).astype(BF)

    near_terms = terms(0)
    away_terms = terms(half)
    near_tail = group_scatter(near_terms[..., UNITS:], "seq", Z_GROUPS).astype(F32)
    sums = exchange_sum(
        jnp.concatenate([away_terms, near_terms[..., :UNITS]], axis=2), "seq", Z_GROUPS
    )
    away_sum = seq_swap(sums[:, : 3 * UNITS].astype(BF), 16).astype(F32)
    hvp = jnp.concatenate([sums[:, 3 * UNITS :], near_tail], axis=1) + away_sum
    return (
        blend(ema_gate, dir_gate, hvp[:, :UNITS]),
        blend(ema_up, dir_up, hvp[:, UNITS : 2 * UNITS]),
        blend(ema_down, dir_down, hvp[:, 2 * UNITS :].T),
    )


def solution(mesh):
    in_specs = (
        P("seq", None),
        P("seq", None),
        P("seq"),
        P(),
        P("seq", "tensor"),
        P("seq", "tensor"),
        P("tensor", "seq"),
        P("seq", "tensor"),
        P("seq", "tensor"),
        P("tensor", "seq"),
        P("seq", "tensor"),
        P("seq", "tensor"),
        P("tensor", "seq"),
    )
    out_specs = (P("seq", "tensor"), P("seq", "tensor"), P("tensor", "seq"))
    return jax.shard_map(
        per_device, mesh=mesh, in_specs=in_specs, out_specs=out_specs, check_vma=False
    )
```

```python
import jax
import jax.numpy as jnp
from jax import lax
from jax.sharding import PartitionSpec as P

gelu_rate = 0.7978845608028654
gelu_cubic = 0.044715
beta_decay = 0.9
norm_eps = 1e-06

NZ = 8
ROWS = 72
UNITS = 288
TALLY = 64
BF = jnp.bfloat16
F32 = jnp.float32


def gelu_parts(pre):
    inner = gelu_rate * (pre + gelu_cubic * pre * pre * pre)
    slope = gelu_rate * (1.0 + 3.0 * gelu_cubic * pre * pre)
    bend = 6.0 * gelu_rate * gelu_cubic * pre
    tanh_val = jnp.tanh(inner)
    sech_sq = 1.0 - tanh_val * tanh_val
    value = 0.5 * pre * (1.0 + tanh_val)
    first = 0.5 * (1.0 + tanh_val) + 0.5 * pre * sech_sq * slope
    second = sech_sq * (slope + 0.5 * pre * (bend - 2.0 * tanh_val * slope * slope))
    return (value, first, second)


def product(left, right):
    return jnp.dot(left, right, preferred_element_type=F32)


def against(left, right):
    return lax.dot_general(left, right, (((1,), (1,)), ((), ())), preferred_element_type=F32)


def over_tokens(left, right):
    return lax.dot_general(left, right, (((0,), (0,)), ((), ())), preferred_element_type=F32)


def blend(ema, probe, hvp):
    return beta_decay * ema + (1.0 - beta_decay) * (probe.astype(F32) * hvp)


def seq_swap(array, bit):
    return lax.ppermute(array, "seq", [(s, s ^ bit) for s in range(32)])


def y_swap(array, bit):
    return lax.ppermute(array, "tensor", [(t, t ^ (bit * 4)) for t in range(16)])


Z_GROUPS = [[y * 16 + z * 2 + c for z in range(8)] for y in range(2) for c in range(2)]
X_GROUPS = [[y * 4 + x for x in range(4)] for y in range(4)]
Y_GROUPS = [[y * 4 + x for y in range(4)] for x in range(4)]


def group_gather(array, axis, groups):
    return lax.all_gather(array, axis, axis_index_groups=groups)


def group_scatter(array, axis, groups):
    return lax.psum_scatter(array, axis, scatter_dimension=0, axis_index_groups=groups)


def group_exchange(array, axis, groups):
    return lax.all_to_all(array, axis, 0, 0, axis_index_groups=groups)


def z_shift(array, by):
    perm = [(s, (s // 16) * 16 + ((s // 2 % 8 + by) % 8) * 2 + s % 2) for s in range(32)]
    return lax.ppermute(array, "seq", perm)


def gather_z(chunk, z):
    r, rows, n = chunk.shape
    h = 128 * ((n + 255) // 256) if n > 128 else n // 2
    buf = jnp.zeros((r, NZ, rows, n), chunk.dtype)

    def put(buf, piece, at, col=0):
        return lax.dynamic_update_slice(buf, piece[:, None], (0, (z + at) % NZ, 0, col))

    buf = put(buf, chunk, 0)
    up = down = chunk
    for k in (1, 2, 3):
        up = z_shift(up, 1)
        down = z_shift(down, -1)
        buf = put(buf, up, NZ - k)
        buf = put(buf, down, k)
    buf = put(buf, z_shift(up[:, :, :h], 1), 4)
    buf = put(buf, z_shift(down[:, :, h:], -1), 4, h)
    return buf


def exchange_sum(parts, axis, groups):
    return jnp.sum(group_exchange(parts, axis, groups).astype(F32), axis=0)


def x_shift(array, by):
    perm = [(t, (t // 4) * 4 + (t % 4 + by) % 4) for t in range(16)]
    return lax.ppermute(array, "tensor", perm)


def scatter_tensor(parts, x, y):
    n = parts[0].shape[1]
    h = n // 2
    parts = [part.reshape(4, 64, n) for part in parts]

    def block(part, at):
        return lax.dynamic_index_in_dim(part, (x + at) % 4, 0, keepdims=False)

    def add(left, right):
        return (left.astype(F32) + right.astype(F32)).astype(BF)

    def onward(part, up, down):
        ahead, behind = block(part, 1), block(part, 3)
        return (
            jnp.concatenate([add(ahead[:, :h], up), ahead[:, h:]], axis=1),
            jnp.concatenate([behind[:, :h], add(behind[:, h:], down)], axis=1),
        )

    far = [block(part, 2) for part in parts]
    ups = [x_shift(f[:, :h], 1) for f in far]
    downs = [x_shift(f[:, h:], -1) for f in far]
    pairs = [onward(*each) for each in zip(parts, ups, downs)]
    ups = [x_shift(up, 1) for up, _ in pairs]
    downs = [x_shift(down, -1) for _, down in pairs]
    low, high = y % 2, y // 2
    sums = [
        (block(part, 0).astype(F32) + up.astype(F32) + down.astype(F32)).reshape(2, 2, 16, n)
        for part, up, down in zip(parts, ups, downs)
    ]
    sent = [lax.dynamic_index_in_dim(s, 1 - low, 1, keepdims=False).astype(BF) for s in sums]
    got = [y_swap(s, 1) for s in sent]
    sums = [
        lax.dynamic_index_in_dim(s, low, 1, keepdims=False) + g.astype(F32)
        for s, g in zip(sums, got)
    ]
    sent = [lax.dynamic_index_in_dim(s, 1 - high, 0, keepdims=False).astype(BF) for s in sums]
    got = [y_swap(s, 2) for s in sent]
    return [
        lax.dynamic_index_in_dim(s, high, 0, keepdims=False) + g.astype(F32)
        for s, g in zip(sums, got)
    ]


def gather_tensor(owns, x, y):
    n = owns[0].shape[1]
    h = n // 2
    low, high = y % 2, y // 2
    others = [y_swap(own, 2) for own in owns]
    pairs = [
        jnp.where(high == 0, jnp.stack([own, other]), jnp.stack([other, own]))
        for own, other in zip(owns, others)
    ]
    others = [y_swap(pair, 1) for pair in pairs]
    rows = [
        jnp.where(
            low == 0, jnp.stack([pair, other], axis=1), jnp.stack([other, pair], axis=1)
        ).reshape(64, n)
        for pair, other in zip(pairs, others)
    ]

    def put(buf, piece, at, col=0):
        return lax.dynamic_update_slice(buf, piece[None], ((x + at) % 4, 0, col))

    ups = [x_shift(r, 1) for r in rows]
    downs = [x_shift(r, -1) for r in rows]
    far_ups = [x_shift(up[:, :h], 1) for up in ups]
    far_downs = [x_shift(down[:, h:], -1) for down in downs]
    result = []
    for own, up, down, far_up, far_down in zip(rows, ups, downs, far_ups, far_downs):
        buf = put(jnp.zeros((4, 64, n), own.dtype), own, 0)
        buf = put(put(buf, up, 3), down, 1)
        buf = put(put(buf, far_up, 2), far_down, 2, h)
        result.append(buf.reshape(256, n))
    return result


def relative(rows, y, c):
    m = rows.shape[0]
    parts = rows.reshape(m, 2, NZ, 2, ROWS).transpose(1, 3, 0, 2, 4).reshape(2, 2, m, NZ * ROWS)
    parts = jnp.where(y == 0, parts, parts[::-1])
    parts = jnp.where(c == 0, parts, parts[:, ::-1])
    return parts.transpose(2, 0, 1, 3).reshape(m, 4 * NZ * ROWS)


def per_device(
    tokens,
    target,
    segment_ids,
    norm_gain,
    w_gate,
    w_up,
    w_down,
    dir_gate,
    dir_up,
    dir_down,
    ema_gate,
    ema_up,
    ema_down,
):
    s = lax.axis_index("seq")
    t = lax.axis_index("tensor")
    yh, z, c = s // 16, (s // 2) % 8, s % 2
    yl, x = t // 4, t % 4

    labels = jnp.arange(32, dtype=jnp.int32)
    onehot = (segment_ids[:, None] == labels[None, :]).astype(F32)

    own_in = jnp.concatenate([w_gate, w_up, dir_gate, dir_up], axis=1)
    tally = jnp.pad(jnp.sum(onehot, axis=0).astype(BF)[None], ((0, ROWS - 1), (0, TALLY - 32)))
    own_out = jnp.concatenate([w_down.T, dir_down.T, tally], axis=1)
    across_in = seq_swap(own_in, 16)
    outs = group_gather(jnp.stack([own_out, seq_swap(own_out, 16)]), "seq", Z_GROUPS)
    ins = gather_z(jnp.stack([own_in, across_in]), z)
    outs_other = seq_swap(outs, 1)
    ins_other = seq_swap(ins, 1)

    wide = tokens.astype(F32)
    scale = lax.rsqrt(jnp.mean(wide * wide, axis=1, keepdims=True) + norm_eps)
    normed = (wide * scale * norm_gain).astype(BF)
    normed = relative(normed, yh, c)

    half = 2 * NZ * ROWS
    near_all, away_all = (
        jnp.stack([ins[i], ins_other[i]]).reshape(half, 4 * UNITS) for i in range(2)
    )
    pre = product(normed[:, :half], near_all) + product(normed[:, half:], away_all)
    gate, upper, gate_dot, upper_dot = (pre[:, i * UNITS : (i + 1) * UNITS] for i in range(4))
    value, first, second = gelu_parts(gate)
    hidden = (value * upper).astype(BF)
    hidden_dot = (first * gate_dot * upper + value * upper_dot).astype(BF)

    outs_all = jnp.stack([outs, outs_other]).transpose(2, 0, 1, 3, 4)
    counts = jnp.sum(outs_all[:, :, :, 0, 2 * UNITS : 2 * UNITS + 32].astype(F32), axis=(0, 1, 2))
    down_all = outs_all[..., : 2 * UNITS].reshape(4 * NZ * ROWS, 2 * UNITS)
    mixed_part = against(hidden, down_all[:, :UNITS]).astype(BF)
    mixed_dot_part = against(jnp.concatenate([hidden_dot, hidden], axis=1), down_all).astype(BF)
    mixed, mixed_dot = scatter_tensor([mixed_part, mixed_dot_part], x, yl)

    at = x * 64 + yl * 16
    my_tokens = relative(lax.dynamic_slice_in_dim(tokens, at, 16, 0), yh, c).astype(F32)
    my_target = relative(lax.dynamic_slice_in_dim(target, at, 16, 0), yh, c).astype(F32)
    my_hot = lax.dynamic_slice_in_dim(onehot, at, 16, 0)
    lengths = jnp.sum(my_hot * counts[None], axis=1, keepdims=True)
    my_grad = ((my_tokens + mixed - my_target) / lengths).astype(BF)
    my_grad_dot = (mixed_dot / lengths).astype(BF)
    grad_out, grad_out_dot = gather_tensor([my_grad, my_grad_dot], x, yl)

    back = product(grad_out, down_all)
    back_dot = product(grad_out_dot, down_all[:, :UNITS])
    grad_hidden = back[:, :UNITS]
    grad_hidden_dot = back_dot + back[:, UNITS:]
    grad_gate_dot = (
        (grad_hidden_dot * upper + grad_hidden * upper_dot) * first
        + grad_hidden * upper * second * gate_dot
    ).astype(BF)
    grad_upper_dot = (grad_hidden_dot * value + grad_hidden * first * gate_dot).astype(BF)
    grads = jnp.concatenate([grad_gate_dot, grad_upper_dot], axis=1)

    def terms(lo):
        rows = slice(lo, lo + half)
        part_in = over_tokens(normed[:, rows], grads).astype(BF)
        part_out = (
            over_tokens(grad_out[:, rows], hidden_dot) + over_tokens(grad_out_dot[:, rows], hidden)
        ).astype(BF)
        part = jnp.concatenate([part_in, part_out], axis=1).reshape(2, NZ, ROWS, 3 * UNITS)
        return (part[0].astype(F32) + seq_swap(part[1], 1).astype(F32)).astype(BF)

    near_terms = terms(0)
    away_terms = terms(half)
    near_tail = group_scatter(near_terms[..., UNITS:], "seq", Z_GROUPS).astype(F32)
    sums = exchange_sum(
        jnp.concatenate([away_terms, near_terms[..., :UNITS]], axis=2), "seq", Z_GROUPS
    )
    away_sum = seq_swap(sums[:, : 3 * UNITS].astype(BF), 16).astype(F32)
    hvp = jnp.concatenate([sums[:, 3 * UNITS :], near_tail], axis=1) + away_sum
    return (
        blend(ema_gate, dir_gate, hvp[:, :UNITS]),
        blend(ema_up, dir_up, hvp[:, UNITS : 2 * UNITS]),
        blend(ema_down, dir_down, hvp[:, 2 * UNITS :].T),
    )


def solution(mesh):
    in_specs = (
        P("seq", None),
        P("seq", None),
        P("seq"),
        P(),
        P("seq", "tensor"),
        P("seq", "tensor"),
        P("tensor", "seq"),
        P("seq", "tensor"),
        P("seq", "tensor"),
        P("tensor", "seq"),
        P("seq", "tensor"),
        P("seq", "tensor"),
        P("tensor", "seq"),
    )
    out_specs = (P("seq", "tensor"), P("seq", "tensor"), P("tensor", "seq"))
    return jax.shard_map(
        per_device, mesh=mesh, in_specs=in_specs, out_specs=out_specs, check_vma=False
    )
```
